128 devices in a mesh: section: 2 (over y_hi), dp: 8 (over z, y_lo), context: 8 (over x, core).
Axes of the slice: x: 4, y: 4 (y_hi: 2, y_lo: 2; y = y_hi * 2 + y_lo), z: 4, core: 2. Of those that a mesh axis runs over, the one named last changes fastest.
Arguments:
- tokens: bfloat16 [16, 1024, 576], P('dp', 'context'), may hold values from -6 to 6
- cotangent: bfloat16 [16, 1024, 576], P('dp', 'context'), may hold values from -6 to 6
- block_map: int32 [16, 16], P('dp'), may hold values from 0 to 15, each once within a row
- attention_gain: bfloat16 [2, 576], P('section', 'dp'), may hold values from 0.099609375 to 1.8984375
- query_weight: bfloat16 [2, 576, 576], P('section', 'dp'), may hold values from -0.25 to 0.25
- keyval_weight: bfloat16 [2, 576, 384], P('section', 'dp'), may hold values from -0.25 to 0.25
- output_weight: bfloat16 [2, 576, 576], P('section', 'dp'), may hold values from -0.75 to 0.75
- feedforward_gain: bfloat16 [2, 576], P('section', 'dp'), may hold values from 0.099609375 to 1.8984375
- gateup_weight: bfloat16 [2, 576, 3072], P('section', 'dp'), may hold values from -0.25 to 0.25
- down_weight: bfloat16 [2, 1536, 576], P('section', 'dp'), may hold values from -0.15625 to 0.15625
Outputs:
- hidden_states: bfloat16 [2, 16, 1024, 576], P('section', 'dp', 'context')
- input_grads: bfloat16 [2, 16, 1024, 576], P('section', 'dp', 'context')
- attention_gain_grads: float32 [2, 576], P('section', 'dp')
- query_grads: float32 [2, 576, 576], P('section', 'dp')
- keyval_grads: float32 [2, 576, 384], P('section', 'dp')
- output_grads: float32 [2, 576, 576], P('section', 'dp')
- feedforward_gain_grads: float32 [2, 576], P('section', 'dp')
- gateup_grads: float32 [2, 576, 3072], P('section', 'dp')
- down_grads: float32 [2, 1536, 576], P('section', 'dp')
The draws below stay inside these ranges and needn't reach their ends.
Inputs may be any that keep to these rules, and one draw needn't show every extreme that they name: Each row is a permutation: stored block j of sequence s holds the sequence's block block_map[s, j].
All inputs are finite; a program needn't handle non-finite values.
Results may differ from the reference program's by a relative error of at most 0.028.
Values may be sent and summed in bfloat16 or wider, within the bound.
A program may use at most 192 MiB of HBM per device.

```python
import jax
import jax.numpy as jnp
from jax import lax

D = 576
HEADS = 9
KV_HEADS = 3
HEAD = 64
FF = 1536
LEN = 1024
LAYERS = 2
SEQS = 16
BLOCKS = 16
BLK = 64
KVW = 192
GROUP = 3


def levels(stream_key, shape, cuts, smallest, largest):
    def one(dim, parts):
        draws = jax.random.uniform(jax.random.fold_in(jax.random.fold_in(stream_key, 6), dim), (parts,), jnp.float32, smallest / len(cuts), largest / len(cuts))
        return jnp.repeat(jnp.exp(draws), shape[dim] // parts).reshape((-1,) + (1,) * (len(shape) - dim - 1))

    level = one(*cuts[0])
    for cut in cuts[1:]:
        level = level * one(*cut)
    return level


def scatter_about(key, shape, width, bound, pieces=(), kind=jnp.bfloat16):
    level = levels(key, shape, pieces, -0.22, 0.18) if pieces else 1.0
    array = jax.random.normal(key, shape, jnp.float32) * width * level
    return jnp.minimum(jnp.maximum(array, -bound), bound).astype(kind)


def setup_inputs(seed: int = 0) -> dict:
    streams_of = jax.random.split(jax.random.key(seed), 11)
    tokens = scatter_about(streams_of[0], (SEQS, LEN, D), 1.0, 6.0, ((0, 8), (1, 8)))
    cotangent = scatter_about(streams_of[1], (SEQS, LEN, D), 1.0, 6.0, ((0, 8), (1, 8)))
    block_map = jax.vmap(lambda own: jax.random.permutation(own, BLOCKS))(jax.random.split(streams_of[2], SEQS)).reshape((SEQS, BLOCKS)).astype(jnp.int32)
    attention_gain = jnp.clip(1.0 + 0.18 * jax.random.normal(streams_of[3], (LAYERS, D), jnp.float32), 0.099609375, 1.8984375).astype(jnp.bfloat16)
    query_weight = scatter_about(streams_of[4], (LAYERS, D, D), D ** -0.5, 0.25, ((0, 2), (1, 8)))
    keyval_weight = scatter_about(streams_of[5], (LAYERS, D, 2 * KVW), D ** -0.5, 0.25, ((0, 2), (1, 8)))
    output_weight = scatter_about(streams_of[6], (LAYERS, D, D), (D // 8) ** -0.5, 0.75, ((0, 2), (1, 8)))
    feedforward_gain = jnp.clip(1.0 + 0.18 * jax.random.normal(streams_of[7], (LAYERS, D), jnp.float32), 0.099609375, 1.8984375).astype(jnp.bfloat16)
    gateup_weight = scatter_about(streams_of[8], (LAYERS, D, 2 * FF), D ** -0.5, 0.25, ((0, 2), (1, 8)))
    down_weight = scatter_about(streams_of[9], (LAYERS, FF, D), FF ** -0.5, 0.15625, ((0, 2), (1, 8)))
    return dict(tokens=tokens, cotangent=cotangent, block_map=block_map, attention_gain=attention_gain, query_weight=query_weight, keyval_weight=keyval_weight, output_weight=output_weight, feedforward_gain=feedforward_gain, gateup_weight=gateup_weight, down_weight=down_weight)


@jax.custom_vjp
def low(v):
    return lax.optimization_barrier(v.astype(jnp.bfloat16)).astype(jnp.float32)

@jax.custom_vjp
def low_back(v):
    return v

def low_keep(v):
    return (low(v), None)

def low_pass(kept, grad):
    return (grad,)

def back_keep(v):
    return (v, None)

def back_low(kept, grad):
    return (low(grad),)
low.defvjp(low_keep, low_pass)
low_back.defvjp(back_keep, back_low)
EPSILON = 1e-05
ROPE_BASE = 100000.0

def matmul(left, right):
    return jnp.dot(left, right, precision=lax.Precision.HIGHEST, preferred_element_type=jnp.float32)

def rms_normed(values, gain):
    return values * lax.rsqrt(lax.optimization_barrier(jnp.mean(values * values, axis=-1, keepdims=True)) + EPSILON) * gain

def rope_tables(positions, head_size):
    half_size = head_size // 2
    freqs = ROPE_BASE ** (-2.0 * jnp.arange(half_size, dtype=jnp.float32) / head_size)
    angles = positions.astype(jnp.float32)[:, None] * freqs[None, :]
    return (jnp.cos(angles), jnp.sin(angles))

def rotate(values, cosine, sine):
    half_size = values.shape[-1] // 2
    first = values[..., :half_size]
    second = values[..., half_size:]
    cosine = cosine[:, None, :]
    sine = sine[:, None, :]
    return jnp.concatenate([first * cosine - second * sine, second * cosine + first * sine], axis=-1)

def layer(inputs, positions, gain_attn, w_query, w_keyval, w_output, gain_ffn, w_gateup, w_down):
    normed = low(rms_normed(inputs, gain_attn))
    queries = low_back(matmul(normed, w_query)).reshape(LEN, HEADS, HEAD)
    keyvals = matmul(normed, w_keyval)
    keys = low_back(keyvals[:, :KVW]).reshape(LEN, KV_HEADS, HEAD)
    values = low(low_back(keyvals[:, KVW:])).reshape(LEN, KV_HEADS, HEAD)
    cosine, sine = rope_tables(positions, HEAD)
    rot_query = low(rotate(queries, cosine, sine)).reshape(LEN, KV_HEADS, GROUP, HEAD)
    rot_keys = low(rotate(keys, cosine, sine))
    scores = low_back(jnp.einsum('lkgd,mkd->kglm', rot_query, rot_keys, precision=lax.Precision.HIGHEST) * HEAD ** (-0.5))
    allowed = positions[None, :] <= positions[:, None]
    probs = low(jax.nn.softmax(jnp.where(allowed[None, None], scores, -jnp.inf), axis=-1))
    attended = jnp.einsum('kglm,mkd->lkgd', probs, values, precision=lax.Precision.HIGHEST).reshape(LEN, D)
    attended = low(low_back(attended))
    mixed = inputs + low_back(matmul(attended, w_output))
    normed_ffn = low(rms_normed(mixed, gain_ffn))
    gateup = matmul(normed_ffn, w_gateup)
    gate_part = low_back(gateup[:, :FF])
    up_part = low_back(gateup[:, FF:])
    hidden = low(jax.nn.silu(gate_part) * up_part)
    return mixed + low_back(matmul(hidden, w_down))

def reference(tokens, cotangent, block_map, attention_gain, query_weight, keyval_weight, output_weight, feedforward_gain, gateup_weight, down_weight):
    params = tuple((w.astype(jnp.float32) for w in (attention_gain, query_weight, keyval_weight, output_weight, feedforward_gain, gateup_weight, down_weight)))
    inputs = tokens.astype(jnp.float32)
    offset = jnp.zeros_like(inputs)

    def run(weights, seq_inputs, seq_offset):

        def per_seq(item):
            first_in, extra, row = item
            positions = (row[:, None] * BLK + jnp.arange(BLK, dtype=jnp.int32)[None, :]).reshape(LEN)
            first_out = layer(first_in, positions, *[w[0] for w in weights])
            second_in = low(low_back(first_out)) + extra
            second_out = layer(second_in, positions, *[w[1] for w in weights])
            return (first_out, second_out)
        return lax.map(jax.checkpoint(per_seq), (seq_inputs, seq_offset, block_map))
    (first_out, second_out), pull = jax.vjp(run, params, inputs, offset)
    grads, grad_tokens, grad_second = pull((jnp.zeros_like(first_out), cotangent.astype(jnp.float32)))
    states = jnp.stack([first_out, second_out]).astype(jnp.bfloat16)
    in_grads = jnp.stack([grad_tokens, grad_second]).astype(jnp.bfloat16)
    return (states, in_grads, grads[0], grads[1], grads[2], grads[3], grads[4], grads[5], grads[6])
```

```python
import jax
import jax.numpy as jnp
from jax import lax
from jax.experimental import pallas as pl
from jax.experimental.pallas import tpu as pltpu
from jax.sharding import Mesh
from jax.sharding import PartitionSpec as P

CONTEXT = ("x", "core")
DP = ("z", "ylo")
EPSILON = 1e-05
ROPE_BASE = 100000.0
BF = jnp.bfloat16
F32 = jnp.float32
R = 128
D = 576
FF = 1536
MESH = pl.DeviceIdType.MESH

NT = (((1,), (1,)), ((), ()))
TN = (((0,), (0,)), ((), ()))


def mm(a, b):
    return jnp.dot(a, b, preferred_element_type=F32)


def mm_nt(a, b):
    return lax.dot_general(a, b, NT, preferred_element_type=F32)


def mm_tn(a, b):
    return lax.dot_general(a, b, TN, preferred_element_type=F32)


SCRATCH = dict(
    Wg=((2, D, 2 * FF), BF),
    Wq=((2, D, 1024), BF),
    Wo=((2, D, D), BF),
    Wd=((2, FF, D), BF),
    Gg=((2, D, 2 * FF), BF),
    Gq=((2, D, 1024), BF),
    Go=((2, D, D), BF),
    Gd=((2, FF, D), BF),
    Rg=((D, 2 * FF), BF),
    Rq=((D, 1024), BF),
    Ro=((D, D), BF),
    Rd=((FF, D), BF),
    Sg=((4, 72, 768), BF),
    Sq=((4, 72, 1024), BF),
    So=((4, 72, D), BF),
    Sd=((4, 192, D), BF),
    Zg=((3, 144, 768), BF),
    Yg=((3, 72, 768), BF),
    Yq=((3, 72, 1024), BF),
    Yo=((3, 72, D), BF),
    Yd=((3, 192, D), BF),
    Xq=((4, 72, 1024), BF),
    Xo=((4, 72, D), BF),
    Xd=((4, 192, D), BF),
    PR=((2, 9, R, 1024), BF),
    GU=((2, R, 2 * FF), BF),
    KV=((2, 1024, 384), BF),
    HID=((2, R, FF), BF),
    NRM=((2, R, D), BF),
    NF=((2, R, D), BF),
    ATT=((2, R, D), BF),
    QS=((2, R, D), BF),
    MIX=((2, R, D), F32),
    HSB=((2, R, D), BF),
    IGB=((2, R, D), BF),
    GGU=((R, 2 * FF), BF),
    ACC=((R, D), F32),
    DKV=((8, 384, R), BF),
    DS=((4, 384, R), BF),
    DT=((4, 384, R), BF),
    DX=((2, 3, 384, R), BF),
    COS=((R, R), F32),
    SIN=((R, R), F32),
    BIAS=((R, 1024), F32),
)
N_SEMS = 224


def mega(tok, cot, bm, wq, wo, wg, wd, hs, ig, oq, oo, og, od, *scratch):
    s = dict(zip(SCRATCH, scratch))
    ss, rs = scratch[-2], scratch[-1]
    sec = lax.axis_index("section")
    z = lax.axis_index("z")
    ylo = lax.axis_index("ylo")
    x = lax.axis_index("x")
    core = lax.axis_index("core")
    y = sec * 2 + ylo
    d = z * 2 + ylo
    ctx = x * 2 + core
    is0, is1 = core == 0, core == 1

    keys = {}

    def sem(key):
        if key not in keys:
            keys[key] = len(keys)
            assert len(keys) <= N_SEMS
        return keys[key]

    def at(dy=0, dz=0, dx=0, dc=0):
        yy = lax.rem(y + dy, 4)
        return (
            lax.div(yy, 2),
            lax.rem(z + dz, 4),
            lax.rem(yy, 2),
            lax.rem(x + dx, 4),
            lax.rem(core + dc, 2),
        )

    def cp(key, src, dst, where):
        i = sem(key)
        return pltpu.make_async_remote_copy(
            src_ref=src,
            dst_ref=dst,
            send_sem=ss.at[i],
            recv_sem=rs.at[i],
            device_id=where,
            device_id_type=MESH,
        )

    def rows(n, i):
        return pl.ds(pl.multiple_of(n * i, 16), n)

    def cols(n, i):
        return pl.ds(pl.multiple_of(n * i, 128), n)

    barrier = pltpu.get_barrier_semaphore()
    peers = [at(dy=k) for k in (1, 2, 3)] + [at(dz=k) for k in (1, 2, 3)]
    peers += [at(dx=k) for k in (1, 2, 3)] + [at(dc=1)]
    for p in peers:
        pl.semaphore_signal(barrier, inc=1, device_id=p, device_id_type=MESH)
    pl.semaphore_wait(barrier, len(peers))

    W = dict(q=s["Wq"], o=s["Wo"], d=s["Wd"])
    S = dict(q=s["Sq"], o=s["So"], d=s["Sd"])
    own = dict(q=wq, o=wo, d=wd)
    OTHERS = ("q", "o", "d")

    def ag_y(m, k):
        if m == "g":
            return cp(("ay", m, k), wg.at[:, cols(768, x)], s["Sg"].at[y], at(dy=k))
        if m == "d":
            return cp(("ay", m, k), wd, s["Wd"].at[sec, rows(192, d)], at(dy=k))
        return cp(("ay", m, k), own[m], S[m].at[y], at(dy=k))

    def ag_z(m, L, k):
        if m == "g":
            part = s["Wg"].at[L, rows(144, z), cols(768, x)]
        elif m == "d":
            part = s["Wd"].at[L, rows(384, z)]
        else:
            part = W[m].at[L, rows(144, z)]
        return cp(("az", m, L, k), part, part, at(dz=k))

    def ag_x(L, k):
        part = s["Wg"].at[L, :, cols(768, x)]
        return cp(("ax", L, k), part, part, at(dx=k))

    def ag_sib_g(L, k):
        part = s["Wg"].at[L, :, cols(768, lax.rem(x + 4 - k, 4))]
        return cp(("asg", L, k), part, part, at(dc=1))

    def ag_sib(m, L):
        part = W[m].at[L]
        return cp(("as", m, L), part, part, at(dc=1))

    def join(m, L):
        buf = s["Sg"] if m == "g" else S[m]
        both = jnp.concatenate([buf[2 * L].astype(F32), buf[2 * L + 1].astype(F32)], axis=0).astype(BF)
        if m == "g":
            s["Wg"][L, rows(144, z), cols(768, x)] = both
        else:
            W[m][L, rows(144, z), :] = both

    @pl.when(is1)
    def _():
        for m in OTHERS:
            for k in (1, 2, 3):
                ag_y(m, k).start()
        s["Sq"][y] = wq[...]
        s["So"][y] = wo[...]
        s["Wd"][sec, rows(192, d), :] = wd[...]

    @pl.when(is0)
    def _():
        for k in (1, 2, 3):
            ag_y("g", k).start()
        s["Sg"][y] = wg[:, cols(768, x)]

    lane = lax.broadcasted_iota(jnp.int32, (R, R), 1)
    row = lax.broadcasted_iota(jnp.int32, (R, R), 0)
    first = row < 64
    pos_t = jnp.where(first, bm[sec, 2 * ctx], bm[sec, 2 * ctx + 1]) * 64 + jnp.where(first, row, row - 64)
    freq = jnp.exp((lane % 32).astype(F32) * F32(-2.0 / 64 * jnp.log(ROPE_BASE)))
    angle = pos_t.astype(F32) * freq
    s["COS"][...] = jnp.cos(angle)
    sine = jnp.sin(angle)
    s["SIN"][...] = jnp.where(lane % 64 < 32, -sine, sine)
    pos_f = pos_t[:, :1].astype(F32)
    for j in range(16):
        u = lax.broadcasted_iota(jnp.int32, (R, 64), 1) + bm[sec, j] * 64
        s["BIAS"][:, 64 * j : 64 * j + 64] = jnp.where(u.astype(F32) <= pos_f, 0.0, -1e30).astype(F32)

    def ag_start_z(L):
        @pl.when(is1)
        def _():
            for m in OTHERS:
                if L == 0:
                    for k in (1, 2, 3):
                        ag_y(m, k).wait_recv()
                if m != "d":
                    join(m, L)
                for k in (1, 2, 3):
                    ag_z(m, L, k).start()

        @pl.when(is0)
        def _():
            if L == 0:
                for k in (1, 2, 3):
                    ag_y("g", k).wait_recv()
            join("g", L)
            for k in (1, 2, 3):
                ag_z("g", L, k).start()

    def ag_fwd_x(L):
        @pl.when(is0)
        def _():
            for k in (1, 2, 3):
                ag_z("g", L, k).wait_recv()
            for k in (1, 2, 3):
                ag_x(L, k).start()
            ag_sib_g(L, 0).start()

    def ag_fwd_sib(m, L):
        @pl.when(is1)
        def _():
            for k in (1, 2, 3):
                ag_z(m, L, k).wait_recv()
            ag_sib(m, L).start()

    def ag_fwd_sib_g(L):
        @pl.when(is0)
        def _():
            for k in (1, 2, 3):
                ag_x(L, k).wait_recv()
                ag_sib_g(L, k).start()

    def need(m, L):
        if m == "g":
            @pl.when(is1)
            def _():
                for k in (0, 1, 2, 3):
                    ag_sib_g(L, k).wait_recv()
        else:
            @pl.when(is0)
            def _():
                ag_sib(m, L).wait_recv()

    def ag_done():
        @pl.when(is1)
        def _():
            for m in OTHERS:
                for k in (1, 2, 3):
                    ag_y(m, k).wait_send()
                for L in (0, 1):
                    for k in (1, 2, 3):
                        ag_z(m, L, k).wait_send()
                    ag_sib(m, L).wait_send()

        @pl.when(is0)
        def _():
            for k in (1, 2, 3):
                ag_y("g", k).wait_send()
            for L in (0, 1):
                for k in (1, 2, 3):
                    ag_z("g", L, k).wait_send()
                    ag_x(L, k).wait_send()
                for k in (0, 1, 2, 3):
                    ag_sib_g(L, k).wait_send()

    def tiled(t, n):
        return jnp.concatenate([t] * n, axis=1)

    def swap(v):
        width = v.shape[1]
        ahead = pltpu.roll(v, width - 32, 1)
        behind = pltpu.roll(v, 32, 1)
        low = lax.broadcasted_iota(jnp.int32, v.shape, 1) % 64 < 32
        return jnp.where(low, ahead, behind)

    def gains(L):
        eye = (
            lax.broadcasted_iota(jnp.int32, (D, D), 0) == lax.broadcasted_iota(jnp.int32, (D, D), 1)
        ).astype(F32).astype(BF)
        both = mm_tn(s["Wq"][L, :, 896:1024], eye)
        return both[64:65], both[65:66]

    def kv_x(L, k):
        part = s["KV"].at[L, rows(R, ctx)]
        return cp(("kx", L, k), part, part, at(dx=k))

    def kv_sib(L, k):
        part = s["KV"].at[L, rows(R, lax.rem(x + 4 - k, 4) * 2 + core)]
        return cp(("ks", L, k), part, part, at(dc=1))

    def hs_send(L):
        return cp("hs", s["HSB"].at[L], hs.at[sec], at(dy=2))

    def ig_send(L):
        return cp("ig", s["IGB"].at[L], ig.at[sec], at(dy=2))

    def forward(L, xin, mid):
        need("q", L)
        gain_a, gain_f = gains(L)
        r = lax.rsqrt(jnp.mean(xin * xin, axis=1, keepdims=True) + EPSILON)
        normed = (xin * r * gain_a).astype(BF)
        s["NRM"][L] = normed
        qkv = mm(normed, s["Wq"][L])
        kq = qkv[:, :768]
        kq = kq * tiled(s["COS"][...], 6) + swap(kq) * tiled(s["SIN"][...], 6)
        s["KV"][L, rows(R, ctx), :] = jnp.concatenate([kq[:, :192], qkv[:, 768:960]], axis=1).astype(BF)
        for k in (1, 2, 3):
            kv_x(L, k).start()
        kv_sib(L, 0).start()
        s["QS"][L] = (kq[:, 192:768] * 0.125).astype(BF)
        mid[0]()
        for k in (1, 2, 3):
            kv_x(L, k).wait_recv()
            kv_sib(L, k).start()
        mid[1]()
        for k in (0, 1, 2, 3):
            kv_sib(L, k).wait_recv()
        outs = []
        for kh in range(3):
            keys_h = s["KV"][L, :, 64 * kh : 64 * kh + 64]
            vals_h = s["KV"][L, :, 192 + 64 * kh : 256 + 64 * kh]
            for h in range(3 * kh, 3 * kh + 3):
                sc = mm_nt(s["QS"][L, :, 64 * h : 64 * h + 64], keys_h) + s["BIAS"][...]
                e = jnp.exp(sc - jnp.max(sc, axis=1, keepdims=True))
                p = (e * (1.0 / jnp.sum(e, axis=1, keepdims=True))).astype(BF)
                s["PR"][L, h] = p
                outs.append(mm(p, vals_h))
        att = jnp.concatenate(outs, axis=1).astype(BF)
        s["ATT"][L] = att
        mid[2]()
        need("o", L)
        mixed = xin + mm(att, s["Wo"][L])
        s["MIX"][L] = mixed
        r = lax.rsqrt(jnp.mean(mixed * mixed, axis=1, keepdims=True) + EPSILON)
        s["NF"][L] = (mixed * r * gain_f).astype(BF)
        mid[3]()
        need("g", L)

        @pl.loop(0, 4)
        def _(q):
            nf = s["NF"][L]
            g = mm(nf, s["Wg"][L, :, cols(384, q)])
            u = mm(nf, s["Wg"][L, :, cols(384, q + 4)])
            s["GU"][L, :, cols(384, q)] = g.astype(BF)
            s["GU"][L, :, cols(384, q + 4)] = u.astype(BF)
            s["HID"][L, :, cols(384, q)] = (g / (1.0 + jnp.exp(-g)) * u).astype(BF)

        mid[4]()
        need("d", L)
        out = (s["MIX"][L] + mm(s["HID"][L], s["Wd"][L])).astype(BF)
        s["HSB"][L] = out

        @pl.when(sec == L)
        def _():
            hs[sec] = out

        @pl.when(sec != L)
        def _():
            hs_send(L).start()

    G = dict(q=s["Gq"], o=s["Go"], d=s["Gd"], g=s["Gg"])
    RAW = dict(q=s["Rq"], o=s["Ro"], d=s["Rd"], g=s["Rg"])
    WALL = dict(W, g=s["Wg"])
    ZN = dict(q=144, o=144, d=384)
    YR = dict(q=s["Yq"], o=s["Yo"], d=s["Yd"])
    XR = dict(q=s["Xq"], o=s["Xo"], d=s["Xd"])
    OUT = dict(q=oq, o=oo, d=od)

    def ra(m, L):
        return RAW[m] if L == 1 else WALL[m].at[1]

    def rz(m, L):
        return G[m].at[0] if L == 1 else RAW[m]

    def g_sib(m, L):
        return cp(("gs", m, L), G[m].at[L], ra(m, L), at(dc=1))

    def grad_out(m, L):
        @pl.when(is1 if m == "g" else is0)
        def _():
            g_sib(m, L).start()

    def add_sib(m, L):
        g_sib(m, L).wait_recv()
        ref, other = G[m].at[L], ra(m, L)
        n = ref.shape[0] // 4

        @pl.loop(0, 4)
        def _(i):
            t = rows(n, i)
            ref[t, :] = (ref[t, :].astype(F32) + other[t, :].astype(F32)).astype(BF)

    def gx(L, k):
        src = s["Gg"].at[L, :, cols(768, lax.rem(x + k, 4))]
        dst = (s["Gg"].at[0] if L == 1 else s["Rg"]).at[:, pl.ds(768 * (k - 1), 768)]
        return cp(("gx", L, k), src, dst, at(dx=k))

    def gz(L, k):
        src = s["Gg"].at[L, rows(144, lax.rem(z + k, 4)), cols(768, x)]
        dst = s["Zg"].at[k - 1] if L == 1 else s["Rg"].at[pl.ds(144 * (k - 1), 144), pl.ds(2304, 768)]
        return cp(("gz", L, k), src, dst, at(dz=k))

    def y_target(L, k):
        yy = lax.rem(y + k, 4)
        return lax.div(yy, 2) == L, lax.rem(yy, 2)

    def gy(L, k):
        _, half = y_target(L, k)
        return cp(("gy", L, k), s["Sg"].at[2 * L + half], s["Yg"].at[k - 1], at(dy=k))

    def gfx(L, k):
        part = og.at[:, cols(768, x)]
        return cp(("gfx", L, k), part, part, at(dx=k))

    def gfs(L, k):
        part = og.at[:, cols(768, lax.rem(x + 4 - k, 4))]
        return cp(("gfs", L, k), part, part, at(dc=1))

    def a1(L):
        @pl.when(is0)
        def _():
            add_sib("g", L)
            for k in (1, 2, 3):
                gx(L, k).start()

    def a2(L):
        @pl.when(is0)
        def _():
            for k in (1, 2, 3):
                gx(L, k).wait_recv()
            other = s["Gg"].at[0] if L == 1 else s["Rg"]

            @pl.loop(0, 4)
            def _(i):
                t = rows(144, i)
                total = s["Gg"][L, t, cols(768, x)].astype(F32)
                for k in range(3):
                    total = total + other[t, 768 * k : 768 * k + 768].astype(F32)
                s["Gg"][L, t, cols(768, x)] = total.astype(BF)

            for k in (1, 2, 3):
                gz(L, k).start()

    def a3(L):
        @pl.when(is0)
        def _():
            for k in (1, 2, 3):
                gz(L, k).wait_recv()
            total = s["Gg"][L, rows(144, z), cols(768, x)].astype(F32)
            for k in range(3):
                other = s["Zg"][k] if L == 1 else s["Rg"][144 * k : 144 * k + 144, 2304:]
                total = total + other.astype(F32)
            s["Sg"][2 * L] = total[:72].astype(BF)
            s["Sg"][2 * L + 1] = total[72:].astype(BF)
            for k in (1, 2, 3):
                @pl.when(y_target(L, k)[0])
                def _():
                    gy(L, k).start()

    def a4(L):
        @pl.when(is0 & (sec == L))
        def _():
            for k in (1, 2, 3):
                gy(L, k).wait_recv()
            total = s["Sg"][2 * L + ylo].astype(F32)
            for k in range(3):
                total = total + s["Yg"][k].astype(F32)
            og[:, cols(768, x)] = total
            for k in (1, 2, 3):
                gfx(L, k).start()
            gfs(L, 0).start()

    def a5(L):
        @pl.when(is0 & (sec == L))
        def _():
            for k in (1, 2, 3):
                gfx(L, k).wait_recv()
                gfs(L, k).start()

    def bz(m, L, k):
        n = ZN[m]
        src = G[m].at[L, rows(n, lax.rem(z + k, 4))]
        dst = rz(m, L).at[pl.ds(n * (k - 1), n)]
        return cp(("bz", m, L, k), src, dst, at(dz=k))

    def by(m, L, k):
        _, half = y_target(L, k)
        return cp(("by", m, L, k), S[m].at[2 * L + half], YR[m].at[k - 1], at(dy=k))

    def bx(m, L, k):
        return cp(("bx", m, L, k), XR[m].at[x], XR[m].at[x], at(dx=k))

    def bf(m, L):
        return cp(("bf", m, L), OUT[m], OUT[m], at(dc=1))

    def b1(m, L):
        @pl.when(is1)
        def _():
            add_sib(m, L)
            for k in (1, 2, 3):
                bz(m, L, k).start()

    def b2(m, L):
        n = ZN[m]

        @pl.when(is1)
        def _():
            for k in (1, 2, 3):
                bz(m, L, k).wait_recv()
            total = G[m][L, rows(n, z), :].astype(F32)
            for k in range(3):
                total = total + rz(m, L)[n * k : n * k + n, :].astype(F32)
            S[m][2 * L] = total[: n // 2].astype(BF)
            S[m][2 * L + 1] = total[n // 2 :].astype(BF)
            for k in (1, 2, 3):
                @pl.when(y_target(L, k)[0])
                def _():
                    by(m, L, k).start()

    def b3(m, L):
        @pl.when(is1 & (sec == L))
        def _():
            for k in (1, 2, 3):
                by(m, L, k).wait_recv()
            total = S[m][2 * L + ylo].astype(F32)
            for k in range(3):
                total = total + YR[m][k].astype(F32)
            XR[m][x] = total.astype(BF)
            for k in (1, 2, 3):
                bx(m, L, k).start()

    def b4(m, L):
        @pl.when(is1 & (sec == L))
        def _():
            for k in (1, 2, 3):
                bx(m, L, k).wait_recv()
            total = XR[m][0].astype(F32)
            for k in range(1, 4):
                total = total + XR[m][k].astype(F32)
            OUT[m][...] = total
            bf(m, L).start()

    def grads_done():
        for L in (0, 1):
            @pl.when(is0)
            def _():
                for m in OTHERS:
                    g_sib(m, L).wait_send()
                for k in (1, 2, 3):
                    gx(L, k).wait_send()
                    gz(L, k).wait_send()

                    @pl.when(y_target(L, k)[0])
                    def _():
                        gy(L, k).wait_send()

            @pl.when(is1)
            def _():
                g_sib("g", L).wait_send()
                for m in OTHERS:
                    for k in (1, 2, 3):
                        bz(m, L, k).wait_send()

                        @pl.when(y_target(L, k)[0])
                        def _():
                            by(m, L, k).wait_send()

            @pl.when(is0 & (sec == L))
            def _():
                for k in (1, 2, 3):
                    gfx(L, k).wait_send()
                for k in range(4):
                    gfs(L, k).wait_send()
                for m in OTHERS:
                    bf(m, L).wait_recv()

            @pl.when(is1 & (sec == L))
            def _():
                for m in OTHERS:
                    for k in (1, 2, 3):
                        bx(m, L, k).wait_send()
                    bf(m, L).wait_send()
                for k in range(4):
                    gfs(L, k).wait_recv()

    def dkv_sib(L, j):
        return cp(("ds", L, j), s["DKV"].at[2 * j + 1 - core], s["DS"].at[j], at(dc=1))

    def dkv_x(L, k):
        return cp(("dx", L, k), s["DT"].at[lax.rem(x + k, 4)], s["DX"].at[L, k - 1], at(dx=k))

    def backward(L, xin, dF, mid):
        gain_a, gain_f = gains(L)
        dlow = dF.astype(BF)
        if L == 1:
            s["IGB"][1] = dlow

        @pl.loop(0, 4)
        def _(q):
            up = s["IGB"][1]
            gh = mm_nt(up, s["Wd"][L, rows(384, q), :])
            g = s["GU"][L, :, cols(384, q)].astype(F32)
            u = s["GU"][L, :, cols(384, q + 4)].astype(F32)
            sig = 1.0 / (1.0 + jnp.exp(-g))
            s["GGU"][:, cols(384, q)] = (gh * u * (sig * (1.0 + g * (1.0 - sig)))).astype(BF)
            s["GGU"][:, cols(384, q + 4)] = (gh * (g * sig)).astype(BF)
            s["Gd"][L, rows(384, q), :] = mm_tn(s["HID"][L, :, cols(384, q)], up).astype(BF)

        grad_out("d", L)
        s["ACC"][...] = jnp.zeros((R, D), F32)

        @pl.loop(0, 4)
        def _(q):
            gg = s["GGU"][:, cols(768, q)]
            s["Gg"][L, :, cols(768, q)] = mm_tn(s["NF"][L], gg).astype(BF)
            s["ACC"][...] += mm_nt(gg, s["Wg"][L, :, cols(768, q)])

        grad_out("g", L)
        gnf = s["ACC"][...]
        mixed = s["MIX"][L]
        r = lax.rsqrt(jnp.mean(mixed * mixed, axis=1, keepdims=True) + EPSILON)
        e = gnf * gain_f
        z_ffn = (gnf * mixed * r).astype(BF)
        gm = dF + r * e - mixed * (r * r * r * jnp.mean(e * mixed, axis=1, keepdims=True))
        gb = gm.astype(BF)
        att = s["ATT"][L]
        s["Go"][L] = mm_tn(att, gb).astype(BF)
        grad_out("o", L)
        ga = mm_nt(gb, s["Wo"][L]).astype(BF)
        mid[0]()
        prod = ga.astype(F32) * att.astype(F32)
        gqs = []
        for kh in range(3):
            keys_h = s["KV"][L, :, 64 * kh : 64 * kh + 64]
            vals_h = s["KV"][L, :, 192 + 64 * kh : 256 + 64 * kh]
            dk = jnp.zeros((64, 1024), F32)
            dv = jnp.zeros((64, 1024), F32)
            for h in range(3 * kh, 3 * kh + 3):
                lanes = slice(64 * h, 64 * h + 64)
                ga_h = ga[:, lanes]
                p = s["PR"][L, h]
                inner = jnp.sum(prod[:, lanes], axis=1, keepdims=True)
                ds = (p.astype(F32) * (mm_nt(ga_h, vals_h) - inner)).astype(BF)
                dv = dv + mm_tn(ga_h, p)
                dk = dk + mm_tn(s["QS"][L, :, lanes], ds)
                gqs.append(mm(ds, keys_h) * 0.125)
            dk, dv = dk.astype(BF), dv.astype(BF)
            for c in range(8):
                s["DKV"][c, 64 * kh : 64 * kh + 64, :] = dk[:, R * c : R * c + R]
                s["DKV"][c, 192 + 64 * kh : 256 + 64 * kh, :] = dv[:, R * c : R * c + R]
        for j in range(4):
            dkv_sib(L, j).start()
        mid[1]()
        for j in range(4):
            dkv_sib(L, j).wait_recv()
            s["DT"][j] = (s["DKV"][2 * j + core].astype(F32) + s["DS"][j].astype(F32)).astype(BF)
        for k in (1, 2, 3):
            dkv_x(L, k).start()
        mid[2]()
        total = s["DT"][x].astype(F32)
        for k in (1, 2, 3):
            dkv_x(L, k).wait_recv()
            total = total + s["DX"][L, k - 1].astype(F32)
        for j in range(4):
            dkv_sib(L, j).wait_send()
        for k in (1, 2, 3):
            dkv_x(L, k).wait_send()
        gkv = total.T
        kq = jnp.concatenate([gkv[:, :192]] + gqs, axis=1)
        kq = kq * tiled(s["COS"][...], 6) - swap(kq) * tiled(s["SIN"][...], 6)
        gall = jnp.concatenate([kq, gkv[:, 192:], jnp.zeros((R, 64), F32)], axis=1).astype(BF)
        r = lax.rsqrt(jnp.mean(xin * xin, axis=1, keepdims=True) + EPSILON)
        gn = mm_nt(gall, s["Wq"][L])
        z_att = (gn * xin * r).astype(BF)
        sel = lax.broadcasted_iota(jnp.int32, (2 * R, 128), 1) - lax.broadcasted_iota(jnp.int32, (2 * R, 128), 0) // R
        tail = mm_tn(jnp.concatenate([z_att, z_ffn], axis=0), (sel == 64).astype(F32).astype(BF))
        gw = mm_tn(s["NRM"][L], gall)
        s["Gq"][L, :, :896] = gw[:, :896].astype(BF)
        s["Gq"][L, :, 896:] = (gw[:, 896:] + tail).astype(BF)
        grad_out("q", L)
        e = gn * gain_a
        dx = gm + r * e - xin * (r * r * r * jnp.mean(e * xin, axis=1, keepdims=True))
        low = dx.astype(BF)
        return low

    def put_ig(L, low):
        s["IGB"][1 if L == 1 else 0] = low

        @pl.when(sec == L)
        def _():
            ig[sec] = low

        @pl.when(sec != L)
        def _():
            ig_send(1 if L == 1 else 0).start()

    ag_start_z(0)
    ag_fwd_x(0)
    ag_fwd_sib("q", 0)

    def f00():
        ag_fwd_sib("o", 0)

    def f01():
        pass

    def f02():
        ag_fwd_sib("d", 0)
        ag_start_z(1)

    def f03():
        ag_fwd_sib_g(0)

    def f04():
        ag_fwd_sib("q", 1)
        ag_fwd_x(1)

    forward(0, tok[sec].astype(F32), (f00, f01, f02, f03, f04))

    def f10():
        ag_fwd_sib("o", 1)
        ag_fwd_sib("d", 1)

    def f13():
        ag_fwd_sib_g(1)

    none = lambda: None
    forward(1, s["HSB"][0].astype(F32), (f10, none, none, f13, none))
    ag_done()
    for L in (0, 1):
        for k in (1, 2, 3):
            kv_x(L, k).wait_send()
        for k in range(4):
            kv_sib(L, k).wait_send()

    def c10():
        a1(1)
        b1("d", 1)

    def c11():
        b1("o", 1)

    def c12():
        b2("d", 1)

    low = backward(1, s["HSB"][0].astype(F32), cot[sec].astype(F32), (c10, c11, c12))
    put_ig(1, low)
    b2("o", 1)
    a2(1)
    b1("q", 1)

    def c00():
        a3(1)
        b3("d", 1)
        b3("o", 1)
        a1(0)
        b1("d", 0)

    def c01():
        b2("q", 1)
        b1("o", 0)
        a4(1)
        b4("d", 1)
        b4("o", 1)

    def c02():
        b3("q", 1)
        a5(1)
        b2("d", 0)

    low = backward(0, tok[sec].astype(F32), s["IGB"][1].astype(F32), (c00, c01, c02))
    put_ig(0, low)
    b4("q", 1)
    b1("q", 0)
    b2("o", 0)
    a2(0)
    b2("q", 0)
    b3("d", 0)
    b3("o", 0)
    a3(0)
    b3("q", 0)
    b4("d", 0)
    b4("o", 0)
    a4(0)
    b4("q", 0)
    a5(0)
    grads_done()

    @pl.when(sec == 0)
    def _():
        hs_send(1).wait()
        ig_send(1).wait()

    @pl.when(sec == 1)
    def _():
        hs_send(0).wait()
        ig_send(0).wait()


def body(tokens, cotangent, block_map, gain_a, w_q, w_kv, w_o, gain_f, w_gu, w_d):
    w_kv, w_q = w_kv[0], w_q[0]
    both = jnp.stack([gain_a[0], gain_f[0]], axis=1)
    wq = jnp.concatenate([w_kv[:, :192], w_q, w_kv[:, 192:], both, jnp.zeros((72, 62), BF)], axis=1)
    vm = pl.BlockSpec(memory_space=pltpu.VMEM)
    hs, ig, oq, oo, og, od = pl.pallas_call(
        mega,
        out_shape=(
            jax.ShapeDtypeStruct((2, R, D), BF),
            jax.ShapeDtypeStruct((2, R, D), BF),
            jax.ShapeDtypeStruct((72, 1024), F32),
            jax.ShapeDtypeStruct((72, D), F32),
            jax.ShapeDtypeStruct((72, 2 * FF), F32),
            jax.ShapeDtypeStruct((192, D), F32),
        ),
        in_specs=[vm, vm, pl.BlockSpec(memory_space=pltpu.SMEM), vm, vm, vm, vm],
        out_specs=(vm,) * 6,
        scratch_shapes=[pltpu.VMEM(shape, dtype) for shape, dtype in SCRATCH.values()]
        + [pltpu.SemaphoreType.DMA((N_SEMS,)), pltpu.SemaphoreType.DMA((N_SEMS,))],
        compiler_params=pltpu.CompilerParams(
            collective_id=0, has_side_effects=True, vmem_limit_bytes=64 * 2**20
        ),
        name="layers",
    )(tokens, cotangent, block_map, wq, w_o[0], w_gu[0], w_d[0])
    return (
        hs[None],
        ig[None],
        oq[None, :, 960],
        oq[None, :, 192:768],
        jnp.concatenate([oq[:, :192], oq[:, 768:960]], axis=1)[None],
        oo[None],
        oq[None, :, 961],
        og[None],
        od[None],
    )


def solution(mesh):
    torus = Mesh(mesh.devices.reshape(2, 4, 2, 4, 2), ("section", "z", "ylo", "x", "core"))
    return jax.shard_map(
        body,
        mesh=torus,
        in_specs=(
            P(DP, CONTEXT, None),
            P(DP, CONTEXT, None),
            P(DP, None),
            P("section", DP),
            P("section", DP, None),
            P("section", DP, None),
            P("section", DP, None),
            P("section", DP),
            P("section", DP, None),
            P("section", DP, None),
        ),
        out_specs=(
            P("section", DP, CONTEXT, None),
            P("section", DP, CONTEXT, None),
            P("section", DP),
            P("section", DP, None),
            P("section", DP, None),
            P("section", DP, None),
            P("section", DP),
            P("section", DP, None),
            P("section", DP, None),
        ),
        check_vma=False,
    )
```

```python
import jax
import jax.numpy as jnp
from jax import lax
from jax.experimental import pallas as pl
from jax.experimental.pallas import tpu as pltpu
from jax.sharding import Mesh
from jax.sharding import PartitionSpec as P

CONTEXT = ("x", "core")
DP = ("z", "ylo")
EPSILON = 1e-05
ROPE_BASE = 100000.0
BF = jnp.bfloat16
F32 = jnp.float32
R = 128
D = 576
FF = 1536
MESH = pl.DeviceIdType.MESH

NT = (((1,), (1,)), ((), ()))
TN = (((0,), (0,)), ((), ()))


def mm(a, b):
    return jnp.dot(a, b, preferred_element_type=F32)


def mm_nt(a, b):
    return lax.dot_general(a, b, NT, preferred_element_type=F32)


def mm_tn(a, b):
    return lax.dot_general(a, b, TN, preferred_element_type=F32)


SCRATCH = dict(
    Wg=((2, D, 2 * FF), BF),
    Wq=((2, D, 1024), BF),
    Wo=((2, D, D), BF),
    Wd=((2, FF, D), BF),
    Gg=((2, D, 2 * FF), BF),
    Gq=((2, D, 1024), BF),
    Go=((2, D, D), BF),
    Gd=((2, FF, 640), BF),
    Rg=((D, 2 * FF), BF),
    Rq=((D, 1024), BF),
    Ro=((D, D), BF),
    Rd=((FF, 640), BF),
    Sg=((4, 72, 768), BF),
    Sq=((4, 72, 1024), BF),
    So=((4, 72, D), BF),
    Yg=((3, 72, 768), BF),
    Yq=((3, 72, 1024), BF),
    Yo=((3, 72, D), BF),
    Yd=((3, 192, 640), BF),
    Xq=((4, 72, 1024), BF),
    Xo=((4, 72, D), BF),
    Xd=((4, 192, 640), BF),
    Xg=((4, 72, 768), BF),
    PR=((2, 9, R, 1024), BF),
    GU=((2, R, 2 * FF), BF),
    KV=((2, 1024, 384), BF),
    HID=((2, R, FF), BF),
    NRM=((2, R, D), BF),
    NF=((2, R, D), BF),
    ATT=((2, R, D), BF),
    QS=((2, R, D), BF),
    MIX=((2, R, D), F32),
    HSB=((2, R, D), BF),
    IGB=((2, R, D), BF),
    ACC=((R, D), F32),
    DKV=((8, 384, R), BF),
    DS=((8, 384, R), BF),
    DX=((2, 3, 2, 384, R), BF),
    SND=((384, R), BF),
    TOT=((384, R), BF),
    COS=((R, R), F32),
    SIN=((R, R), F32),
    BIAS=((R, 1024), F32),
)
N_SEMS = 256


def mega(tok, cot, bm, wq, wo, wg, wd, hs, ig, oq, oo, og, od, *scratch):
    s = dict(zip(SCRATCH, scratch))
    ss, rs, free = scratch[-3:]
    sec = lax.axis_index("section")
    z = lax.axis_index("z")
    ylo = lax.axis_index("ylo")
    x = lax.axis_index("x")
    core = lax.axis_index("core")
    y = sec * 2 + ylo
    d = z * 2 + ylo
    ctx = x * 2 + core
    is0, is1 = core == 0, core == 1

    keys = {}

    def sem(key):
        if key not in keys:
            keys[key] = len(keys)
            assert len(keys) <= N_SEMS
        return keys[key]

    def at(dy=0, dz=0, dx=0, dc=0):
        yy = lax.rem(y + dy, 4)
        return (
            lax.div(yy, 2),
            lax.rem(z + dz, 4),
            lax.rem(yy, 2),
            lax.rem(x + dx, 4),
            lax.rem(core + dc, 2),
        )

    def cp(key, src, dst, where):
        i = sem(key)
        return pltpu.make_async_remote_copy(
            src_ref=src,
            dst_ref=dst,
            send_sem=ss.at[i],
            recv_sem=rs.at[i],
            device_id=where,
            device_id_type=MESH,
        )

    def rows(n, i):
        return pl.ds(pl.multiple_of(n * i, 16), n)

    def cols(n, i):
        return pl.ds(pl.multiple_of(n * i, 128), n)

    barrier = pltpu.get_barrier_semaphore()
    peers = [at(dy=k) for k in (1, 2, 3)] + [at(dz=k) for k in (1, 2, 3)]
    peers += [at(dx=k) for k in (1, 2, 3)] + [at(dc=1)]
    for p in peers:
        pl.semaphore_signal(barrier, inc=1, device_id=p, device_id_type=MESH)
    pl.semaphore_wait(barrier, len(peers))

    W = dict(q=s["Wq"], o=s["Wo"], d=s["Wd"])
    S = dict(q=s["Sq"], o=s["So"])
    own = dict(q=wq, o=wo, d=wd)
    OTHERS = ("q", "o", "d")

    def ag_y(m, k):
        if m == "g":
            return cp(("ay", m, k), wg.at[:, cols(768, x)], s["Sg"].at[y], at(dy=k))
        return cp(("ay", m, k), own[m], S[m].at[y], at(dy=k))

    def down_z(k):
        return cp(("dz", k), wd, s["Wd"].at[sec, rows(192, d)], at(dz=k))

    def down_y(k, zz):
        part = s["Wd"].at[sec, rows(192, 2 * zz + ylo)]
        return cp(("dy", k, zz), part, part, at(dy=k))

    def from_section(k):
        return lax.div(lax.rem(y + 4 - k, 4), 2)

    def ag_z(m, L, k):
        if m == "g":
            part = s["Wg"].at[L, rows(144, z), cols(768, x)]
        else:
            part = W[m].at[L, rows(144, z)]
        return cp(("az", m, L, k), part, part, at(dz=k))

    def ag_x(L, k):
        part = s["Wg"].at[L, :, cols(768, x)]
        return cp(("ax", L, k), part, part, at(dx=k))

    def ag_x2(L, k):
        part = s["Wg"].at[L, pl.ds(0 if k == 1 else 288, 288), cols(768, lax.rem(x + 4 - k, 4))]
        return cp(("ax2", L, k), part, part, at(dx=k))

    def ag_sib_g(L, k):
        part = s["Wg"].at[L, :, cols(768, lax.rem(x + 4 - k, 4))]
        return cp(("asg", L, k), part, part, at(dc=1))

    def ag_sib(m, L):
        part = W[m].at[L]
        return cp(("as", m, L), part, part, at(dc=1))

    def join(m, L):
        buf = s["Sg"] if m == "g" else S[m]
        both = jnp.concatenate([buf[2 * L + h].astype(F32) for h in (0, 1)], axis=0).astype(BF)
        if m == "g":
            s["Wg"][L, rows(144, z), cols(768, x)] = both
        else:
            W[m][L, rows(144, z), :] = both

    @pl.when(is1)
    def _():
        for k in (1, 2, 3):
            ag_y("q", k).start()
        for k in (1, 2, 3):
            down_z(k).start()
        s["Sq"][y] = wq[...]
        s["So"][y] = wo[...]
        s["Wd"][sec, rows(192, d), :] = wd[...]

    @pl.when(is0)
    def _():
        for k in (1, 2, 3):
            ag_y("g", k).start()
        s["Sg"][y] = wg[:, cols(768, x)]

    def tables():
        lane = lax.broadcasted_iota(jnp.int32, (R, R), 1)
        row = lax.broadcasted_iota(jnp.int32, (R, R), 0)
        first = row < 64
        pos_t = jnp.where(first, bm[sec, 2 * ctx], bm[sec, 2 * ctx + 1]) * 64 + jnp.where(first, row, row - 64)
        freq = jnp.exp((lane % 32).astype(F32) * F32(-2.0 / 64 * jnp.log(ROPE_BASE)))
        angle = pos_t.astype(F32) * freq
        s["COS"][...] = jnp.cos(angle)
        sine = jnp.sin(angle)
        s["SIN"][...] = jnp.where(lane % 64 < 32, -sine, sine)
        pos_f = pos_t[:, :1].astype(F32)
        for j in range(16):
            u = lax.broadcasted_iota(jnp.int32, (R, 64), 1) + bm[sec, j] * 64
            s["BIAS"][:, 64 * j : 64 * j + 64] = jnp.where(u.astype(F32) <= pos_f, 0.0, -1e30).astype(F32)

    def ag_start_o():
        @pl.when(is1)
        def _():
            for k in (1, 2, 3):
                ag_y("o", k).start()

    def wait_y(m):
        for k in (1, 2, 3):
            ag_y(m, k).wait_recv()

    def ag_start_z(m, L):
        @pl.when(is0 if m == "g" else is1)
        def _():
            if L == 0:
                wait_y(m)
            join(m, L)
            if m == "q" and L == 0:
                pl.semaphore_wait(free.at[3], 1)
            for k in (1, 2, 3):
                ag_z(m, L, k).start()

    def down_send(L):
        @pl.when(is1 & (sec == L))
        def _():
            for k in (1, 2, 3):
                down_z(k).wait_recv()
            for zz in range(4):
                for k in (1, 2, 3):
                    down_y(k, zz).start()

    def down_have(L):
        @pl.when(is1)
        def _():
            for k in (1, 2, 3):
                @pl.when(from_section(k) == L)
                def _():
                    for zz in range(4):
                        down_y(k, zz).wait_recv()
            ag_sib("d", L).start()

    def ag_fwd_x(L):
        @pl.when(is0)
        def _():
            for k in (1, 2, 3):
                ag_z("g", L, k).wait_recv()
            for k in (1, 3):
                ag_x(L, k).start()
            if L == 0:
                pl.semaphore_signal(free.at[3], inc=1, device_id=at(dc=1), device_id_type=MESH)
            ag_sib_g(L, 0).start()

    def ag_fwd_x2(L):
        @pl.when(is0)
        def _():
            for k in (1, 3):
                ag_x(L, k).wait_recv()
                ag_x2(L, k).start()
            for k in (1, 3):
                ag_sib_g(L, k).start()

    def ag_fwd_sib(m, L):
        @pl.when(is1)
        def _():
            for k in (1, 2, 3):
                ag_z(m, L, k).wait_recv()
            ag_sib(m, L).start()

    def ag_fwd_sib_g(L):
        @pl.when(is0)
        def _():
            for k in (1, 3):
                ag_x2(L, k).wait_recv()
            ag_sib_g(L, 2).start()

    def need(m, L):
        if m == "g":
            @pl.when(is1)
            def _():
                for k in (0, 1, 2, 3):
                    ag_sib_g(L, k).wait_recv()
        else:
            @pl.when(is0)
            def _():
                ag_sib(m, L).wait_recv()

    def ag_done():
        @pl.when(is1)
        def _():
            for k in (1, 2, 3):
                down_z(k).wait_send()
                for zz in range(4):
                    down_y(k, zz).wait_send()
            for m in OTHERS:
                if m != "d":
                    for k in (1, 2, 3):
                        ag_y(m, k).wait_send()
                for L in (0, 1):
                    if m != "d":
                        for k in (1, 2, 3):
                            ag_z(m, L, k).wait_send()
                    ag_sib(m, L).wait_send()

        @pl.when(is0)
        def _():
            for k in (1, 2, 3):
                ag_y("g", k).wait_send()
            for L in (0, 1):
                for k in (1, 2, 3):
                    ag_z("g", L, k).wait_send()
                for k in (1, 3):
                    ag_x(L, k).wait_send()
                    ag_x2(L, k).wait_send()
                for k in (0, 1, 2, 3):
                    ag_sib_g(L, k).wait_send()

    def tiled(t, n):
        return jnp.concatenate([t] * n, axis=1)

    def swap(v):
        width = v.shape[1]
        ahead = pltpu.roll(v, width - 32, 1)
        behind = pltpu.roll(v, 32, 1)
        low = lax.broadcasted_iota(jnp.int32, v.shape, 1) % 64 < 32
        return jnp.where(low, ahead, behind)

    def gains(L):
        eye = (
            lax.broadcasted_iota(jnp.int32, (D, D), 0) == lax.broadcasted_iota(jnp.int32, (D, D), 1)
        ).astype(F32).astype(BF)
        both = mm_tn(s["Wq"][L, :, 896:1024], eye)
        return both[64:65], both[65:66]

    def kv_up(L):
        part = s["KV"].at[L, rows(R, ctx)]
        return cp(("ku", L), part, part, at(dc=1))

    def kv_x(L, who, k):
        part = s["KV"].at[L, rows(R, 2 * x + who)]
        return cp(("kx", L, who, k), part, part, at(dx=k))

    def kv_down(L, k):
        part = s["KV"].at[L, rows(2 * R, lax.rem(x + 4 - k, 4))]
        return cp(("kd", L, k), part, part, at(dc=1))

    def kv_done(L):
        kv_up(L).wait_send()

        @pl.when(is1)
        def _():
            for k in (1, 2, 3):
                for who in (0, 1):
                    kv_x(L, who, k).wait_send()
                kv_down(L, k).wait_send()

    def hs_send(L):
        return cp("hs", s["HSB"].at[L], hs.at[sec], at(dy=2))

    def ig_send(L):
        return cp("ig", s["IGB"].at[L], ig.at[sec], at(dy=2))

    def forward(L, xin, mid):
        need("q", L)
        gain_a, gain_f = gains(L)
        r = lax.rsqrt(jnp.mean(xin * xin, axis=1, keepdims=True) + EPSILON)
        normed = (xin * r * gain_a).astype(BF)
        s["NRM"][L] = normed
        qkv = mm(normed, s["Wq"][L])
        kq = qkv[:, :768]
        kq = kq * tiled(s["COS"][...], 6) + swap(kq) * tiled(s["SIN"][...], 6)
        s["KV"][L, rows(R, ctx), :] = jnp.concatenate([kq[:, :192], qkv[:, 768:960]], axis=1).astype(BF)
        kv_up(L).start()

        @pl.when(is1)
        def _():
            for k in (1, 2, 3):
                kv_x(L, 1, k).start()
            kv_up(L).wait_recv()
            for k in (1, 2, 3):
                kv_x(L, 0, k).start()

        s["QS"][L] = (kq[:, 192:768] * 0.125).astype(BF)
        mid[0]()

        @pl.when(is1)
        def _():
            for k in (1, 2, 3):
                for who in (0, 1):
                    kv_x(L, who, k).wait_recv()
                kv_down(L, k).start()

        mid[1]()

        @pl.when(is0)
        def _():
            kv_up(L).wait_recv()
            for k in (1, 2, 3):
                kv_down(L, k).wait_recv()

        outs = []
        for kh in range(3):
            keys_h = s["KV"][L, :, 64 * kh : 64 * kh + 64]
            vals_h = s["KV"][L, :, 192 + 64 * kh : 256 + 64 * kh]
            for h in range(3 * kh, 3 * kh + 3):
                sc = mm_nt(s["QS"][L, :, 64 * h : 64 * h + 64], keys_h) + s["BIAS"][...]
                e = jnp.exp(sc - jnp.max(sc, axis=1, keepdims=True))
                p = (e * (1.0 / jnp.sum(e, axis=1, keepdims=True))).astype(BF)
                s["PR"][L, h] = p
                outs.append(mm(p, vals_h))
        att = jnp.concatenate(outs, axis=1).astype(BF)
        s["ATT"][L] = att
        mid[2]()
        need("o", L)
        mixed = xin + mm(att, s["Wo"][L])
        s["MIX"][L] = mixed
        r = lax.rsqrt(jnp.mean(mixed * mixed, axis=1, keepdims=True) + EPSILON)
        s["NF"][L] = (mixed * r * gain_f).astype(BF)
        mid[3]()
        need("g", L)

        @pl.loop(0, 4)
        def _(q):
            nf = s["NF"][L]
            g = mm(nf, s["Wg"][L, :, cols(384, q)])
            u = mm(nf, s["Wg"][L, :, cols(384, q + 4)])
            s["GU"][L, :, cols(384, q)] = g.astype(BF)
            s["GU"][L, :, cols(384, q + 4)] = u.astype(BF)
            s["HID"][L, :, cols(384, q)] = (g / (1.0 + jnp.exp(-g)) * u).astype(BF)

        mid[4]()
        need("d", L)
        out = (s["MIX"][L] + mm(s["HID"][L], s["Wd"][L])).astype(BF)
        s["HSB"][L] = out

        @pl.when(sec == L)
        def _():
            hs[sec] = out

        @pl.when(sec != L)
        def _():
            hs_send(L).start()

    G = dict(q=s["Gq"], o=s["Go"], d=s["Gd"], g=s["Gg"])
    RAW = dict(q=s["Rq"], o=s["Ro"], d=s["Rd"], g=s["Rg"])
    WALL = dict(W, g=s["Wg"])
    ZN = dict(q=144, o=144, d=384)
    YR = dict(q=s["Yq"], o=s["Yo"])
    XR = dict(q=s["Xq"], o=s["Xo"], d=s["Xd"])
    OUT = dict(q=oq, o=oo, d=od)

    def ra(m, L):
        return RAW[m] if L == 1 or m in "gd" else WALL[m].at[1]

    def rz(m, L):
        return G[m].at[0] if L == 1 else RAW[m]

    def g_sib(m, L):
        return cp(("gs", m, L), G[m].at[L], ra(m, L), at(dc=1))

    parts = {(m, L): [sem(("part", m, L, i)) for i in range(4)][0] for m in "gd" for L in (0, 1)}

    def g_part(m, L, i):
        at_i = (slice(None), cols(768, i)) if m == "g" else (rows(384, i),)
        j = parts[m, L] + i
        return pltpu.make_async_remote_copy(
            src_ref=G[m].at[(L, *at_i)],
            dst_ref=ra(m, L).at[at_i],
            send_sem=ss.at[j],
            recv_sem=rs.at[j],
            device_id=at(dc=1),
            device_id_type=MESH,
        )

    def grad_out(m, L, i=None):
        @pl.when(is1 if m == "g" else is0)
        def _():
            (g_sib(m, L) if i is None else g_part(m, L, i)).start()

    def add_sib(m, L):
        if m not in "gd":
            g_sib(m, L).wait_recv()
        ref, other = G[m].at[L], ra(m, L)

        @pl.loop(0, 4)
        def _(i):
            if m in "gd":
                g_part(m, L, i).wait_recv()
            t = (slice(None), cols(768, i)) if m == "g" else (rows(ref.shape[0] // 4, i), slice(None))
            ref[t] = (ref[t].astype(F32) + other[t].astype(F32)).astype(BF)

    def gx(L, step, k):
        toward = lax.rem(x + k, 4)
        top = pl.ds(0, 288)
        bottom = pl.ds(288, 288)
        if step == 0:
            half, col, slot = (top if k == 1 else bottom), lax.rem(x + 2, 4), 0
        elif step == 1:
            half, col, slot = (bottom if k == 1 else top), toward, (1 if k == 1 else 2)
        else:
            half, col, slot = (top if k == 1 else bottom), toward, (1 if k == 1 else 2)
        src = s["Gg"].at[L, half, cols(768, col)]
        dst = s["Wg"].at[1, half, pl.ds(768 * slot, 768)]
        return cp(("gx", L, step, k), src, dst, at(dx=k))

    def gz(L, k):
        src = s["Gg"].at[L, rows(144, lax.rem(z + k, 4)), cols(768, x)]
        dst = s["Wg"].at[1, pl.ds(144 * (k - 1), 144), pl.ds(2304, 768)]
        return cp(("gz", L, k), src, dst, at(dz=k))

    def y_target(L, k):
        yy = lax.rem(y + k, 4)
        return lax.div(yy, 2) == L, lax.rem(yy, 2)

    def gy(L, k):
        _, ours = y_target(L, k)
        return cp(("gy", L, k), s["Sg"].at[2 * L + ours], s["Yg"].at[k - 1], at(dy=k))

    def gfx(L, k):
        return cp(("gfx", L, k), s["Xg"].at[x], s["Xg"].at[x], at(dx=k))

    def gfs(L, k):
        part = s["Xg"].at[lax.rem(x + 4 - k, 4)]
        return cp(("gfs", L, k), part, part, at(dc=1))

    def og_put():
        for i in range(4):
            og[:, 768 * i : 768 * i + 768] = s["Xg"][i].astype(F32)

    def give(i, **way):
        for k in (1, 2, 3):
            where = at(**{axis: k for axis in way})
            pl.semaphore_signal(free.at[i], inc=1, device_id=where, device_id_type=MESH)

    def a0(L):
        @pl.when(is0)
        def _():
            add_sib("g", L)

    def a1(L):
        @pl.when(is0)
        def _():
            pl.semaphore_wait(free.at[L], 2)
            for k in (1, 3):
                gx(L, 0, k).start()

    def a1b(L):
        @pl.when(is0)
        def _():
            for k in (1, 3):
                gx(L, 1, k).start()
            for k in (1, 3):
                half = pl.ds(0 if k == 1 else 288, 288)
                at_cols = cols(768, lax.rem(x + k, 4))
                gx(L, 0, k).wait_recv()
                both = s["Gg"][L, half, at_cols].astype(F32) + s["Wg"][1, half, :768].astype(F32)
                s["Gg"][L, half, at_cols] = both.astype(BF)
                gx(L, 2, k).start()

    def a2(L):
        @pl.when(is0)
        def _():
            for k in (1, 3):
                gx(L, 1, k).wait_recv()
                gx(L, 2, k).wait_recv()

            @pl.loop(0, 4)
            def _(i):
                t = rows(144, i)
                total = s["Gg"][L, t, cols(768, x)].astype(F32)
                for k in (1, 2):
                    total = total + s["Wg"][1, t, 768 * k : 768 * k + 768].astype(F32)
                s["Gg"][L, t, cols(768, x)] = total.astype(BF)

            if L == 1:
                give2(0)
            pl.semaphore_wait(free.at[4 + L], 3)
            for k in (1, 2, 3):
                gz(L, k).start()

    def a3(L):
        @pl.when(is0)
        def _():
            for k in (1, 2, 3):
                gz(L, k).wait_recv()
            total = s["Gg"][L, rows(144, z), cols(768, x)].astype(F32)
            for k in range(3):
                total = total + s["Wg"][1, 144 * k : 144 * k + 144, 2304:].astype(F32)
            s["Sg"][2 * L] = total[:72].astype(BF)
            s["Sg"][2 * L + 1] = total[72:].astype(BF)
            if L == 1:
                give(4, dz=1)
            for k in (1, 2, 3):
                @pl.when(y_target(L, k)[0])
                def _():
                    gy(L, k).start()

    def a4(L):
        @pl.when(is0 & (sec == L))
        def _():
            for k in (1, 2, 3):
                gy(L, k).wait_recv()
            total = s["Sg"][2 * L + ylo].astype(F32)
            for k in range(3):
                total = total + s["Yg"][k].astype(F32)
            s["Xg"][x] = total.astype(BF)
            for k in (1, 2, 3):
                gfx(L, k).start()
            gfs(L, 0).start()

    def a5(L):
        @pl.when(is0 & (sec == L))
        def _():
            for k in (1, 2, 3):
                gfx(L, k).wait_recv()
                gfs(L, k).start()
            og_put()

    def give2(i):
        for k in (1, 3):
            pl.semaphore_signal(free.at[i], inc=1, device_id=at(dx=k), device_id_type=MESH)

    def bz(m, L, k):
        n = ZN[m]
        src = G[m].at[L, rows(n, lax.rem(z + k, 4))]
        dst = rz(m, L).at[pl.ds(n * (k - 1), n)]
        return cp(("bz", m, L, k), src, dst, at(dz=k))

    def by(m, L, k):
        _, half = y_target(L, k)
        return cp(("by", m, L, k), S[m].at[2 * L + half], YR[m].at[k - 1], at(dy=k))

    def bx(m, L, k):
        return cp(("bx", m, L, k), XR[m].at[x], XR[m].at[x], at(dx=k))

    def bf(m, L):
        return cp(("bf", m, L), OUT[m], OUT[m], at(dc=1))

    def hy(L, k, zz):
        _, half = y_target(L, k)
        src = s["Gd"].at[L, rows(192, 2 * zz + half)]
        dst = s["Wg"].at[1, pl.ds(192 * (k - 1), 192), pl.ds(768 * zz, 640)]
        return cp(("hy", L, k, zz), src, dst, at(dy=k))

    def hz(L, k):
        src = s["Gd"].at[L, rows(192, 2 * lax.rem(z + k, 4) + ylo)]
        return cp(("hz", L, k), src, s["Yd"].at[k - 1], at(dz=k))

    def d1(L):
        @pl.when(is1)
        def _():
            add_sib("d", L)
            if L == 1:
                pl.semaphore_wait(free.at[2], 3)
            for k in (1, 2, 3):
                @pl.when(y_target(L, k)[0])
                def _():
                    for zz in range(4):
                        hy(L, k, zz).start()

    def d2(L):
        @pl.when(is1 & (sec == L))
        def _():
            for k in (1, 2, 3):
                for zz in range(4):
                    hy(L, k, zz).wait_recv()
            for zz in range(4):
                t = rows(192, 2 * zz + ylo)
                total = s["Gd"][L, t, :].astype(F32)
                for k in range(3):
                    total = total + s["Wg"][1, 192 * k : 192 * k + 192, 768 * zz : 768 * zz + 640].astype(F32)
                s["Gd"][L, t, :] = total.astype(BF)
            for k in (1, 2, 3):
                hz(L, k).start()

    def d3(L):
        @pl.when(is1 & (sec == L))
        def _():
            for k in (1, 2, 3):
                hz(L, k).wait_recv()
            total = s["Gd"][L, rows(192, d), :].astype(F32)
            for k in range(3):
                total = total + s["Yd"][k].astype(F32)
            s["Xd"][x] = total.astype(BF)
            for k in (1, 2, 3):
                bx("d", L, k).start()

    def b1(m, L):
        @pl.when(is1)
        def _():
            add_sib(m, L)
            for k in (1, 2, 3):
                bz(m, L, k).start()

    def b2(m, L):
        n = ZN[m]

        @pl.when(is1)
        def _():
            for k in (1, 2, 3):
                bz(m, L, k).wait_recv()
            total = G[m][L, rows(n, z), :].astype(F32)
            for k in range(3):
                total = total + rz(m, L)[n * k : n * k + n, :].astype(F32)
            S[m][2 * L] = total[: n // 2].astype(BF)
            S[m][2 * L + 1] = total[n // 2 :].astype(BF)
            for k in (1, 2, 3):
                @pl.when(y_target(L, k)[0])
                def _():
                    by(m, L, k).start()

    def b3(m, L):
        @pl.when(is1 & (sec == L))
        def _():
            for k in (1, 2, 3):
                by(m, L, k).wait_recv()
            total = S[m][2 * L + ylo].astype(F32)
            for k in range(3):
                total = total + YR[m][k].astype(F32)
            XR[m][x] = total.astype(BF)
            for k in (1, 2, 3):
                bx(m, L, k).start()

    def b4(m, L):
        @pl.when(is1 & (sec == L))
        def _():
            for k in (1, 2, 3):
                bx(m, L, k).wait_recv()
            total = XR[m][0].astype(F32)
            for k in range(1, 4):
                total = total + XR[m][k].astype(F32)
            OUT[m][...] = total[:, : OUT[m].shape[1]]
            bf(m, L).start()

    def grads_done():
        for L in (0, 1):
            @pl.when(is0)
            def _():
                for i in range(4):
                    g_part("d", L, i).wait_send()
                for m in ("q", "o"):
                    g_sib(m, L).wait_send()
                for k in (1, 3):
                    for step in range(3):
                        gx(L, step, k).wait_send()
                for k in (1, 2, 3):
                    gz(L, k).wait_send()

                    @pl.when(y_target(L, k)[0])
                    def _():
                        gy(L, k).wait_send()

            @pl.when(is1)
            def _():
                for i in range(4):
                    g_part("g", L, i).wait_send()
                for k in (1, 2, 3):
                    @pl.when(y_target(L, k)[0])
                    def _():
                        for zz in range(4):
                            hy(L, k, zz).wait_send()
                for m in ("q", "o"):
                    for k in (1, 2, 3):
                        bz(m, L, k).wait_send()

                        @pl.when(y_target(L, k)[0])
                        def _():
                            by(m, L, k).wait_send()

            @pl.when(is0 & (sec == L))
            def _():
                for k in (1, 2, 3):
                    gfx(L, k).wait_send()
                for k in range(4):
                    gfs(L, k).wait_send()
                for m in OTHERS:
                    bf(m, L).wait_recv()

            @pl.when(is1 & (sec == L))
            def _():
                for k in (1, 2, 3):
                    hz(L, k).wait_send()
                for m in OTHERS:
                    for k in (1, 2, 3):
                        bx(m, L, k).wait_send()
                    bf(m, L).wait_send()
                for k in range(4):
                    gfs(L, k).wait_recv()
                og_put()

    def dkv_up(L):
        return cp(("du", L), s["DKV"], s["DS"], at(dc=1))

    def dkv_x(L, k):
        src = s["DKV"].at[pl.ds(2 * lax.rem(x + k, 4), 2)]
        return cp(("dx", L, k), src, s["DX"].at[L, k - 1], at(dx=k))

    def dkv_down(L):
        return cp(("dd", L), s["SND"], s["TOT"], at(dc=1))

    def backward(L, xin, dF, mid):
        gain_a, gain_f = gains(L)
        dlow = dF.astype(BF)
        if L == 1:
            s["IGB"][1] = dlow

        @pl.loop(0, 4)
        def _(q):
            up = s["IGB"][1]
            gh = mm_nt(up, s["Wd"][L, rows(384, q), :])
            g = s["GU"][L, :, cols(384, q)].astype(F32)
            u = s["GU"][L, :, cols(384, q + 4)].astype(F32)
            sig = 1.0 / (1.0 + jnp.exp(-g))
            s["GU"][L, :, cols(384, q)] = (gh * u * (sig * (1.0 + g * (1.0 - sig)))).astype(BF)
            s["GU"][L, :, cols(384, q + 4)] = (gh * (g * sig)).astype(BF)
            s["Gd"][L, rows(384, q), :D] = mm_tn(s["HID"][L, :, cols(384, q)], up).astype(BF)
            grad_out("d", L, q)

        s["ACC"][...] = jnp.zeros((R, D), F32)

        @pl.loop(0, 4)
        def _(q):
            gg = s["GU"][L, :, cols(768, q)]
            s["Gg"][L, :, cols(768, q)] = mm_tn(s["NF"][L], gg).astype(BF)
            grad_out("g", L, q)
            s["ACC"][...] += mm_nt(gg, s["Wg"][L, :, cols(768, q)])

        if L == 1:
            @pl.when(is0)
            def _():
                give2(1)
                give(5, dz=1)

            @pl.when(is1)
            def _():
                give(2, dy=1)
        gnf = s["ACC"][...]
        mixed = s["MIX"][L]
        r = lax.rsqrt(jnp.mean(mixed * mixed, axis=1, keepdims=True) + EPSILON)
        e = gnf * gain_f
        z_ffn = (gnf * mixed * r).astype(BF)
        gm = dF + r * e - mixed * (r * r * r * jnp.mean(e * mixed, axis=1, keepdims=True))
        gb = gm.astype(BF)
        att = s["ATT"][L]
        s["Go"][L] = mm_tn(att, gb).astype(BF)
        grad_out("o", L)
        ga = mm_nt(gb, s["Wo"][L]).astype(BF)
        mid[0]()
        prod = ga.astype(F32) * att.astype(F32)
        gqs = []
        for kh in range(3):
            keys_h = s["KV"][L, :, 64 * kh : 64 * kh + 64]
            vals_h = s["KV"][L, :, 192 + 64 * kh : 256 + 64 * kh]
            dk = jnp.zeros((64, 1024), F32)
            dv = jnp.zeros((64, 1024), F32)
            for h in range(3 * kh, 3 * kh + 3):
                lanes = slice(64 * h, 64 * h + 64)
                ga_h = ga[:, lanes]
                p = s["PR"][L, h]
                inner = jnp.sum(prod[:, lanes], axis=1, keepdims=True)
                ds = (p.astype(F32) * (mm_nt(ga_h, vals_h) - inner)).astype(BF)
                dv = dv + mm_tn(ga_h, p)
                dk = dk + mm_tn(s["QS"][L, :, lanes], ds)
                gqs.append(mm(ds, keys_h) * 0.125)
            dk, dv = dk.astype(BF), dv.astype(BF)
            for c in range(8):
                s["DKV"][c, 64 * kh : 64 * kh + 64, :] = dk[:, R * c : R * c + R]
                s["DKV"][c, 192 + 64 * kh : 256 + 64 * kh, :] = dv[:, R * c : R * c + R]
        mid[1]()

        @pl.when(is0)
        def _():
            dkv_up(L).start()

        @pl.when(is1)
        def _():
            dkv_up(L).wait_recv()
            s["DKV"][...] = (s["DKV"][...].astype(F32) + s["DS"][...].astype(F32)).astype(BF)
            for k in (1, 2, 3):
                dkv_x(L, k).start()

        mid[2]()

        @pl.when(is1)
        def _():
            total = s["DKV"][pl.ds(2 * x, 2)].astype(F32)
            for k in (1, 2, 3):
                dkv_x(L, k).wait_recv()
                total = total + s["DX"][L, k - 1].astype(F32)
            s["SND"][...] = total[0].astype(BF)
            s["TOT"][...] = total[1].astype(BF)
            dkv_down(L).start()
            for k in (1, 2, 3):
                dkv_x(L, k).wait_send()
            dkv_down(L).wait_send()

        @pl.when(is0)
        def _():
            dkv_down(L).wait_recv()
            dkv_up(L).wait_send()

        mid[3]()
        total = s["TOT"][...].astype(F32)
        gkv = total.T
        kq = jnp.concatenate([gkv[:, :192]] + gqs, axis=1)
        kq = kq * tiled(s["COS"][...], 6) - swap(kq) * tiled(s["SIN"][...], 6)
        gall = jnp.concatenate([kq, gkv[:, 192:], jnp.zeros((R, 64), F32)], axis=1).astype(BF)
        r = lax.rsqrt(jnp.mean(xin * xin, axis=1, keepdims=True) + EPSILON)
        gn = mm_nt(gall, s["Wq"][L])
        z_att = (gn * xin * r).astype(BF)
        sel = lax.broadcasted_iota(jnp.int32, (2 * R, 128), 1) - lax.broadcasted_iota(jnp.int32, (2 * R, 128), 0) // R
        tail = mm_tn(jnp.concatenate([z_att, z_ffn], axis=0), (sel == 64).astype(F32).astype(BF))
        gw = mm_tn(s["NRM"][L], gall)
        s["Gq"][L, :, :896] = gw[:, :896].astype(BF)
        s["Gq"][L, :, 896:] = (gw[:, 896:] + tail).astype(BF)
        grad_out("q", L)
        e = gn * gain_a
        dx = gm + r * e - xin * (r * r * r * jnp.mean(e * xin, axis=1, keepdims=True))
        low = dx.astype(BF)
        return low

    def put_ig(L, low):
        s["IGB"][1 if L == 1 else 0] = low

        @pl.when(sec == L)
        def _():
            ig[sec] = low

        @pl.when(sec != L)
        def _():
            ig_send(1 if L == 1 else 0).start()

    none = lambda: None
    ag_start_z("g", 0)
    down_send(0)
    ag_start_z("q", 0)
    ag_start_o()
    tables()
    ag_fwd_x(0)
    ag_fwd_sib("q", 0)

    def f00():
        ag_start_z("g", 1)
        ag_start_z("o", 0)
        ag_start_z("q", 1)
        ag_fwd_x2(0)

    def f01():
        ag_start_z("o", 1)

    def f02():
        ag_fwd_sib("o", 0)
        down_have(0)
        down_send(1)

    def f03():
        ag_fwd_sib_g(0)
        ag_fwd_x(1)
        ag_fwd_sib("q", 1)

    forward(0, tok[sec].astype(F32), (f00, f01, f02, f03, none))

    def f10():
        ag_fwd_x2(1)

    def f12():
        ag_fwd_sib("o", 1)

    def f13():
        ag_fwd_sib_g(1)
        down_have(1)

    forward(1, s["HSB"][0].astype(F32), (f10, none, f12, f13, none))
    ag_done()
    kv_done(0)
    kv_done(1)

    def c11():
        a0(1)
        a1(1)
        d1(1)
        b1("o", 1)

    def c12():
        a1b(1)

    low = backward(1, s["HSB"][0].astype(F32), cot[sec].astype(F32), (none, c11, c12, none))
    put_ig(1, low)
    b2("o", 1)

    def c00():
        a2(1)
        b1("q", 1)

    def c01():
        a0(0)
        a1(0)
        d1(0)
        b1("o", 0)

    def c02():
        a1b(0)
        d2(1)
        b2("q", 1)

    def c03():
        a3(1)

    low = backward(0, tok[sec].astype(F32), s["IGB"][1].astype(F32), (c00, c01, c02, c03))
    put_ig(0, low)
    b1("q", 0)
    d2(0)
    b2("o", 0)
    a2(0)
    a4(1)
    d3(1)
    b3("o", 1)
    b3("q", 1)
    b2("q", 0)
    a3(0)
    d3(0)
    b3("o", 0)
    b3("q", 0)
    a5(1)
    b4("d", 1)
    b4("o", 1)
    b4("q", 1)
    a4(0)
    b4("d", 0)
    b4("o", 0)
    b4("q", 0)
    a5(0)
    grads_done()

    @pl.when(sec == 0)
    def _():
        hs_send(1).wait()
        ig_send(1).wait()

    @pl.when(sec == 1)
    def _():
        hs_send(0).wait()
        ig_send(0).wait()


def body(tokens, cotangent, block_map, gain_a, w_q, w_kv, w_o, gain_f, w_gu, w_d):
    w_kv, w_q = w_kv[0], w_q[0]
    both = jnp.stack([gain_a[0], gain_f[0]], axis=1)
    wq = jnp.concatenate([w_kv[:, :192], w_q, w_kv[:, 192:], both, jnp.zeros((72, 62), BF)], axis=1)
    vm = pl.BlockSpec(memory_space=pltpu.VMEM)
    hs, ig, oq, oo, og, od = pl.pallas_call(
        mega,
        out_shape=(
            jax.ShapeDtypeStruct((2, R, D), BF),
            jax.ShapeDtypeStruct((2, R, D), BF),
            jax.ShapeDtypeStruct((72, 1024), F32),
            jax.ShapeDtypeStruct((72, D), F32),
            jax.ShapeDtypeStruct((72, 2 * FF), F32),
            jax.ShapeDtypeStruct((192, D), F32),
        ),
        in_specs=[vm, vm, pl.BlockSpec(memory_space=pltpu.SMEM), vm, vm, vm, vm],
        out_specs=(vm,) * 6,
        scratch_shapes=[pltpu.VMEM(shape, dtype) for shape, dtype in SCRATCH.values()]
        + [pltpu.SemaphoreType.DMA((N_SEMS,))] * 2
        + [pltpu.SemaphoreType.REGULAR((6,))],
        compiler_params=pltpu.CompilerParams(
            collective_id=0, has_side_effects=True, vmem_limit_bytes=64 * 2**20
        ),
        name="layers",
    )(tokens, cotangent, block_map, wq, w_o[0], w_gu[0], w_d[0])
    return (
        hs[None],
        ig[None],
        oq[None, :, 960],
        oq[None, :, 192:768],
        jnp.concatenate([oq[:, :192], oq[:, 768:960]], axis=1)[None],
        oo[None],
        oq[None, :, 961],
        og[None],
        od[None],
    )


def solution(mesh):
    torus = Mesh(mesh.devices.reshape(2, 4, 2, 4, 2), ("section", "z", "ylo", "x", "core"))
    return jax.shard_map(
        body,
        mesh=torus,
        in_specs=(
            P(DP, CONTEXT, None),
            P(DP, CONTEXT, None),
            P(DP, None),
            P("section", DP),
            P("section", DP, None),
            P("section", DP, None),
            P("section", DP, None),
            P("section", DP),
            P("section", DP, None),
            P("section", DP, None),
        ),
        out_specs=(
            P("section", DP, CONTEXT, None),
            P("section", DP, CONTEXT, None),
            P("section", DP),
            P("section", DP, None),
            P("section", DP, None),
            P("section", DP, None),
            P("section", DP),
            P("section", DP, None),
            P("section", DP, None),
        ),
        check_vma=False,
    )
```

```python
import jax
import jax.numpy as jnp
from jax import lax
from jax.experimental import pallas as pl
from jax.experimental.pallas import tpu as pltpu
from jax.sharding import Mesh
from jax.sharding import PartitionSpec as P

CONTEXT = ("x", "core")
DP = ("z", "ylo")
EPSILON = 1e-05
ROPE_BASE = 100000.0
BF = jnp.bfloat16
F32 = jnp.float32
R = 128
D = 576
FF = 1536
MESH = pl.DeviceIdType.MESH

NT = (((1,), (1,)), ((), ()))
TN = (((0,), (0,)), ((), ()))


def mm(a, b):
    return jnp.dot(a, b, preferred_element_type=F32)


def mm_nt(a, b):
    return lax.dot_general(a, b, NT, preferred_element_type=F32)


def mm_tn(a, b):
    return lax.dot_general(a, b, TN, preferred_element_type=F32)


SCRATCH = dict(
    Wg=((2, D, 2 * FF), BF),
    Wq=((2, D, 1024), BF),
    Wo=((2, D, D), BF),
    Wd=((2, FF, D), BF),
    Gg=((2, D, 2 * FF), BF),
    Gq=((2, D, 1024), BF),
    Go=((2, D, D), BF),
    Gd=((2, FF, 640), BF),
    Rg=((D, 2 * FF), BF),
    Rq=((D, 1024), BF),
    Ro=((D, D), BF),
    Rd=((FF, 640), BF),
    Sg=((4, 72, 768), BF),
    Sq=((4, 72, 1024), BF),
    So=((4, 72, D), BF),
    Yg=((3, 72, 768), BF),
    Yq=((3, 72, 1024), BF),
    Yo=((3, 72, D), BF),
    Yd=((3, 192, 640), BF),
    Xq=((4, 72, 1024), BF),
    Xo=((4, 72, D), BF),
    Xd=((4, 192, 640), BF),
    Xg=((4, 72, 768), BF),
    PR=((2, 9, R, 1024), BF),
    GU=((2, R, 2 * FF), BF),
    KV=((2, 1024, 384), BF),
    HID=((2, R, FF), BF),
    NRM=((2, R, D), BF),
    NF=((2, R, D), BF),
    ATT=((2, R, D), BF),
    QS=((2, R, D), BF),
    MIX=((2, R, D), F32),
    HSB=((R, D), BF),
    IGB=((R, D), BF),
    ACC=((R, D), F32),
    DKV=((8, 384, R), BF),
    DS=((8, 384, R), BF),
    DX=((2, 3, 2, 384, R), BF),
    SND=((384, R), BF),
    TOT=((384, R), BF),
    COS=((R, R), F32),
    SIN=((R, R), F32),
    BIAS=((R, 1024), F32),
    TOK=((R, D), BF),
    TOKT=((D, R), BF),
    COTT=((D, R), BF),
    HST=((D, R), BF),
    HST1=((D, R), BF),
    IGT=((D, R), BF),
    IGT1=((D, R), BF),
    IQ=((72, D), BF),
    IKV=((72, 384), BF),
    VG=((72, 2 * FF), F32),
    VD=((192, D), F32),
    VO=((72, D), F32),
    VQ=((72, 1024), F32),
    VQ2=((72, D), F32),
    VKV=((72, 384), F32),
    VGA=((1, 72), F32),
    VGF=((1, 72), F32),
)
N_SEMS = 256


def mega(tok, cot, bm, gain_a, gain_f, wq, wkv, wo, wg, wd, hs, ig, o_ga, o_q, o_kv, o_o, o_gf, o_g, o_d, *scratch):
    s = dict(zip(SCRATCH, scratch))
    ss, rs, free, ls = scratch[-4:]
    sec = lax.axis_index("section")
    z = lax.axis_index("z")
    ylo = lax.axis_index("ylo")
    x = lax.axis_index("x")
    core = lax.axis_index("core")
    y = sec * 2 + ylo
    d = z * 2 + ylo
    ctx = x * 2 + core
    is0, is1 = core == 0, core == 1

    keys = {}

    def sem(key):
        if key not in keys:
            keys[key] = len(keys)
            assert len(keys) <= N_SEMS
        return keys[key]

    def at(dy=0, dz=0, dx=0, dc=0):
        yy = lax.rem(y + dy, 4)
        return (
            lax.div(yy, 2),
            lax.rem(z + dz, 4),
            lax.rem(yy, 2),
            lax.rem(x + dx, 4),
            lax.rem(core + dc, 2),
        )

    def cp(key, src, dst, where):
        i = sem(key)
        return pltpu.make_async_remote_copy(
            src_ref=src,
            dst_ref=dst,
            send_sem=ss.at[i],
            recv_sem=rs.at[i],
            device_id=where,
            device_id_type=MESH,
        )

    def rows(n, i):
        return pl.ds(pl.multiple_of(n * i, 16), n)

    def cols(n, i):
        return pl.ds(pl.multiple_of(n * i, 128), n)

    def here(i, src, dst):
        return pltpu.make_async_copy(src, dst, ls.at[i])

    load = dict(
        tok=here(0, tok.at[sec], s["TOKT"]),
        cot=here(1, cot.at[sec], s["COTT"]),
        q=here(2, wq.at[0], s["IQ"]),
        kv=here(3, wkv.at[0], s["IKV"]),
        o=here(4, wo.at[0], s["So"].at[y]),
        d=here(5, wd.at[0], s["Wd"].at[sec, rows(192, d)]),
        g=here(6, wg.at[0, :, cols(768, x)], s["Sg"].at[y]),
    )
    store = dict(
        g=here(7, s["VG"], o_g.at[0]),
        d=here(8, s["VD"], o_d.at[0]),
        o=here(9, s["VO"], o_o.at[0]),
        q=here(10, s["VQ2"], o_q.at[0]),
        kv=here(11, s["VKV"], o_kv.at[0]),
        ga=here(12, s["VGA"], o_ga),
        gf=here(13, s["VGF"], o_gf),
        hs0=here(14, s["HST"], hs.at[0, sec]),
        hs1=here(14, s["HST1"], hs.at[0, sec]),
        ig0=here(15, s["IGT"], ig.at[0, sec]),
        ig1=here(15, s["IGT1"], ig.at[0, sec]),
    )

    load["tok"].start()

    @pl.when(is1)
    def _():
        for m in ("q", "kv", "d", "o"):
            load[m].start()

    @pl.when(is0)
    def _():
        load["g"].start()

    load["cot"].start()

    barrier = pltpu.get_barrier_semaphore()
    peers = [at(dy=k) for k in (1, 2, 3)] + [at(dz=k) for k in (1, 2, 3)]
    peers += [at(dx=k) for k in (1, 2, 3)] + [at(dc=1)]
    for p in peers:
        pl.semaphore_signal(barrier, inc=1, device_id=p, device_id_type=MESH)
    pl.semaphore_wait(barrier, len(peers))

    W = dict(q=s["Wq"], o=s["Wo"], d=s["Wd"])
    S = dict(q=s["Sq"], o=s["So"])
    own = dict(q=s["Sq"].at[y], o=wo.at[0])
    OTHERS = ("q", "o", "d")

    def ag_y(m, k):
        if m == "g":
            return cp(("ay", m, k), wg.at[0, :, cols(768, x)], s["Sg"].at[y], at(dy=k))
        return cp(("ay", m, k), own[m], S[m].at[y], at(dy=k))

    def down_z(k):
        return cp(("dz", k), wd.at[0], s["Wd"].at[sec, rows(192, d)], at(dz=k))

    def down_y(k, zz):
        part = s["Wd"].at[sec, rows(192, 2 * zz + ylo)]
        return cp(("dy", k, zz), part, part, at(dy=k))

    def from_section(k):
        return lax.div(lax.rem(y + 4 - k, 4), 2)

    def ag_z(m, L, k):
        if m == "g":
            part = s["Wg"].at[L, rows(144, z), cols(768, x)]
        else:
            part = W[m].at[L, rows(144, z)]
        return cp(("az", m, L, k), part, part, at(dz=k))

    def ag_x(L, k):
        part = s["Wg"].at[L, :, cols(768, x)]
        return cp(("ax", L, k), part, part, at(dx=k))

    def ag_x2(L, k):
        part = s["Wg"].at[L, pl.ds(0 if k == 1 else 288, 288), cols(768, lax.rem(x + 4 - k, 4))]
        return cp(("ax2", L, k), part, part, at(dx=k))

    def ag_sib_g(L, k):
        part = s["Wg"].at[L, :, cols(768, lax.rem(x + 4 - k, 4))]
        return cp(("asg", L, k), part, part, at(dc=1))

    def ag_sib(m, L):
        part = W[m].at[L]
        return cp(("as", m, L), part, part, at(dc=1))

    def join(m, L):
        buf = s["Sg"] if m == "g" else S[m]
        both = jnp.concatenate([buf[2 * L + h].astype(F32) for h in (0, 1)], axis=0).astype(BF)
        if m == "g":
            s["Wg"][L, rows(144, z), cols(768, x)] = both
        else:
            W[m][L, rows(144, z), :] = both

    @pl.when(is0)
    def _():
        for k in (1, 2, 3):
            ag_y("g", k).start()
        load["g"].wait()

    @pl.when(is1)
    def _():
        eye = lax.broadcasted_iota(jnp.int32, (72, 72), 0) == lax.broadcasted_iota(jnp.int32, (72, 72), 1)
        gain = [jnp.sum(jnp.where(eye, g[...].astype(F32), 0.0), axis=1, keepdims=True) for g in (gain_a, gain_f)]
        load["q"].wait()
        load["kv"].wait()
        kv = s["IKV"][...].astype(F32)
        parts = [kv[:, :192], s["IQ"][...].astype(F32), kv[:, 192:], *gain, jnp.zeros((72, 62), F32)]
        s["Sq"][y] = jnp.concatenate(parts, axis=1).astype(BF)
        for k in (1, 2, 3):
            ag_y("q", k).start()
        for k in (1, 2, 3):
            down_z(k).start()
        load["d"].wait()
        load["o"].wait()

    def tables():
        lane = lax.broadcasted_iota(jnp.int32, (R, R), 1)
        row = lax.broadcasted_iota(jnp.int32, (R, R), 0)
        first = row < 64
        pos_t = jnp.where(first, bm[sec, 2 * ctx], bm[sec, 2 * ctx + 1]) * 64 + jnp.where(first, row, row - 64)
        freq = jnp.exp((lane % 32).astype(F32) * F32(-2.0 / 64 * jnp.log(ROPE_BASE)))
        angle = pos_t.astype(F32) * freq
        s["COS"][...] = jnp.cos(angle)
        sine = jnp.sin(angle)
        s["SIN"][...] = jnp.where(lane % 64 < 32, -sine, sine)
        pos_f = pos_t[:, :1].astype(F32)
        for j in range(16):
            u = lax.broadcasted_iota(jnp.int32, (R, 64), 1) + bm[sec, j] * 64
            s["BIAS"][:, 64 * j : 64 * j + 64] = jnp.where(u.astype(F32) <= pos_f, 0.0, -1e30).astype(F32)

    def ag_start_o():
        @pl.when(is1)
        def _():
            for k in (1, 2, 3):
                ag_y("o", k).start()

    def wait_y(m):
        for k in (1, 2, 3):
            ag_y(m, k).wait_recv()

    def ag_start_z(m, L):
        @pl.when(is0 if m == "g" else is1)
        def _():
            if L == 0:
                wait_y(m)
            join(m, L)
            for k in (1, 2, 3):
                ag_z(m, L, k).start()

    def down_send(L):
        @pl.when(is1 & (sec == L))
        def _():
            for k in (1, 2, 3):
                down_z(k).wait_recv()
            for zz in range(4):
                for k in (1, 2, 3):
                    down_y(k, zz).start()

    def down_have(L):
        @pl.when(is1)
        def _():
            for k in (1, 2, 3):
                @pl.when(from_section(k) == L)
                def _():
                    for zz in range(4):
                        down_y(k, zz).wait_recv()
            ag_sib("d", L).start()

    def ag_fwd_x(L):
        @pl.when(is0)
        def _():
            for k in (1, 2, 3):
                ag_z("g", L, k).wait_recv()
            for k in (1, 3):
                ag_x(L, k).start()
            ag_sib_g(L, 0).start()

    def ag_fwd_x2(L):
        @pl.when(is0)
        def _():
            for k in (1, 3):
                ag_x(L, k).wait_recv()
                ag_x2(L, k).start()
            for k in (1, 3):
                ag_sib_g(L, k).start()

    def ag_fwd_sib(m, L):
        @pl.when(is1)
        def _():
            for k in (1, 2, 3):
                ag_z(m, L, k).wait_recv()
            ag_sib(m, L).start()

    def ag_fwd_sib_g(L):
        @pl.when(is0)
        def _():
            for k in (1, 3):
                ag_x2(L, k).wait_recv()
            ag_sib_g(L, 2).start()

    def need(m, L):
        if m == "g":
            @pl.when(is1)
            def _():
                for k in (0, 1, 2, 3):
                    ag_sib_g(L, k).wait_recv()
        else:
            @pl.when(is0)
            def _():
                ag_sib(m, L).wait_recv()

    def ag_done():
        @pl.when(is1)
        def _():
            for k in (1, 2, 3):
                down_z(k).wait_send()
                for zz in range(4):
                    down_y(k, zz).wait_send()
            for m in OTHERS:
                if m != "d":
                    for k in (1, 2, 3):
                        ag_y(m, k).wait_send()
                for L in (0, 1):
                    if m != "d":
                        for k in (1, 2, 3):
                            ag_z(m, L, k).wait_send()
                    ag_sib(m, L).wait_send()

        @pl.when(is0)
        def _():
            for k in (1, 2, 3):
                ag_y("g", k).wait_send()
            for L in (0, 1):
                for k in (1, 2, 3):
                    ag_z("g", L, k).wait_send()
                for k in (1, 3):
                    ag_x(L, k).wait_send()
                    ag_x2(L, k).wait_send()
                for k in (0, 1, 2, 3):
                    ag_sib_g(L, k).wait_send()

    def tiled(t, n):
        return jnp.concatenate([t] * n, axis=1)

    def swap(v):
        width = v.shape[1]
        ahead = pltpu.roll(v, width - 32, 1)
        behind = pltpu.roll(v, 32, 1)
        low = lax.broadcasted_iota(jnp.int32, v.shape, 1) % 64 < 32
        return jnp.where(low, ahead, behind)

    def gains(L):
        eye = (
            lax.broadcasted_iota(jnp.int32, (D, D), 0) == lax.broadcasted_iota(jnp.int32, (D, D), 1)
        ).astype(F32).astype(BF)
        both = mm_tn(s["Wq"][L, :, 896:1024], eye)
        return both[64:65], both[65:66]

    def kv_up(L):
        part = s["KV"].at[L, rows(R, ctx)]
        return cp(("ku", L), part, part, at(dc=1))

    def kv_x(L, who, k):
        part = s["KV"].at[L, rows(R, 2 * x + who)]
        return cp(("kx", L, who, k), part, part, at(dx=k))

    def kv_down(L, k):
        part = s["KV"].at[L, rows(2 * R, lax.rem(x + 4 - k, 4))]
        return cp(("kd", L, k), part, part, at(dc=1))

    def kv_done(L):
        kv_up(L).wait_send()

        @pl.when(is1)
        def _():
            for k in (1, 2, 3):
                for who in (0, 1):
                    kv_x(L, who, k).wait_send()
                kv_down(L, k).wait_send()

    def hs_send(L):
        return cp("hs", s["HST1" if L == 1 else "HST"], hs.at[0, sec], at(dy=2))

    def ig_send(L):
        return cp("ig", s["IGT1" if L == 1 else "IGT"], ig.at[0, sec], at(dy=2))

    def forward(L, xin, mid):
        need("q", L)
        gain_a, gain_f = gains(L)
        r = lax.rsqrt(jnp.mean(xin * xin, axis=1, keepdims=True) + EPSILON)
        normed = (xin * r * gain_a).astype(BF)
        s["NRM"][L] = normed
        qkv = mm(normed, s["Wq"][L])
        kq = qkv[:, :768]
        kq = kq * tiled(s["COS"][...], 6) + swap(kq) * tiled(s["SIN"][...], 6)
        s["KV"][L, rows(R, ctx), :] = jnp.concatenate([kq[:, :192], qkv[:, 768:960]], axis=1).astype(BF)
        kv_up(L).start()

        @pl.when(is1)
        def _():
            for k in (1, 2, 3):
                kv_x(L, 1, k).start()
            kv_up(L).wait_recv()
            for k in (1, 2, 3):
                kv_x(L, 0, k).start()

        s["QS"][L] = (kq[:, 192:768] * 0.125).astype(BF)
        mid[0]()

        @pl.when(is1)
        def _():
            for k in (1, 2, 3):
                for who in (0, 1):
                    kv_x(L, who, k).wait_recv()
                kv_down(L, k).start()

        mid[1]()

        @pl.when(is0)
        def _():
            kv_up(L).wait_recv()
            for k in (1, 2, 3):
                kv_down(L, k).wait_recv()

        mid[5]()
        outs = []
        for kh in range(3):
            keys_h = s["KV"][L, :, 64 * kh : 64 * kh + 64]
            vals_h = s["KV"][L, :, 192 + 64 * kh : 256 + 64 * kh]
            for h in range(3 * kh, 3 * kh + 3):
                sc = mm_nt(s["QS"][L, :, 64 * h : 64 * h + 64], keys_h) + s["BIAS"][...]
                e = jnp.exp(sc - jnp.max(sc, axis=1, keepdims=True))
                p = (e * (1.0 / jnp.sum(e, axis=1, keepdims=True))).astype(BF)
                s["PR"][L, h] = p
                outs.append(mm(p, vals_h))
        att = jnp.concatenate(outs, axis=1).astype(BF)
        s["ATT"][L] = att
        mid[2]()
        need("o", L)
        mixed = xin + mm(att, s["Wo"][L])
        s["MIX"][L] = mixed
        r = lax.rsqrt(jnp.mean(mixed * mixed, axis=1, keepdims=True) + EPSILON)
        s["NF"][L] = (mixed * r * gain_f).astype(BF)
        mid[3]()
        need("g", L)

        @pl.loop(0, 4)
        def _(q):
            nf = s["NF"][L]
            g = mm(nf, s["Wg"][L, :, cols(384, q)])
            u = mm(nf, s["Wg"][L, :, cols(384, q + 4)])
            s["GU"][L, :, cols(384, q)] = g.astype(BF)
            s["GU"][L, :, cols(384, q + 4)] = u.astype(BF)
            s["HID"][L, :, cols(384, q)] = (g / (1.0 + jnp.exp(-g)) * u).astype(BF)

        mid[4]()
        need("d", L)
        out = (s["MIX"][L] + mm(s["HID"][L], s["Wd"][L])).astype(BF)
        if L == 0:
            s["HSB"][...] = out
        s["HST1" if L == 1 else "HST"][...] = out.astype(F32).T.astype(BF)

        @pl.when(sec == L)
        def _():
            store["hs%d" % L].start()

        @pl.when(sec != L)
        def _():
            hs_send(L).start()

    G = dict(q=s["Gq"], o=s["Go"], d=s["Gd"], g=s["Gg"])
    RAW = dict(q=s["Rq"], o=s["Ro"], d=s["Rd"], g=s["Rg"])
    WALL = dict(W, g=s["Wg"])
    ZN = dict(q=144, o=144, d=384)
    YR = dict(q=s["Yq"], o=s["Yo"])
    XR = dict(q=s["Xq"], o=s["Xo"], d=s["Xd"])
    OUT = dict(q=s["VQ"], o=s["VO"], d=s["VD"])

    def ra(m, L):
        return RAW[m] if L == 1 or m in "gd" else WALL[m].at[1]

    def rz(m, L):
        return G[m].at[0] if L == 1 else RAW[m]

    def g_sib(m, L):
        return cp(("gs", m, L), G[m].at[L], ra(m, L), at(dc=1))

    parts = {(m, L): [sem(("part", m, L, i)) for i in range(4)][0] for m in "gd" for L in (0, 1)}

    def g_part(m, L, i):
        at_i = (slice(None), cols(768, i)) if m == "g" else (rows(384, i),)
        j = parts[m, L] + i
        return pltpu.make_async_remote_copy(
            src_ref=G[m].at[(L, *at_i)],
            dst_ref=ra(m, L).at[at_i],
            send_sem=ss.at[j],
            recv_sem=rs.at[j],
            device_id=at(dc=1),
            device_id_type=MESH,
        )

    def grad_out(m, L, i=None):
        @pl.when(is1 if m == "g" else is0)
        def _():
            (g_sib(m, L) if i is None else g_part(m, L, i)).start()

    def add_sib(m, L):
        if m not in "gd":
            g_sib(m, L).wait_recv()
        ref, other = G[m].at[L], ra(m, L)

        @pl.loop(0, 4)
        def _(i):
            if m in "gd":
                g_part(m, L, i).wait_recv()
            t = (slice(None), cols(768, i)) if m == "g" else (rows(ref.shape[0] // 4, i), slice(None))
            ref[t] = (ref[t].astype(F32) + other[t].astype(F32)).astype(BF)

    def gx(L, step, k):
        toward = lax.rem(x + k, 4)
        top = pl.ds(0, 288)
        bottom = pl.ds(288, 288)
        if step == 0:
            half, col, slot = (top if k == 1 else bottom), lax.rem(x + 2, 4), 0
        elif step == 1:
            half, col, slot = (bottom if k == 1 else top), toward, (1 if k == 1 else 2)
        else:
            half, col, slot = (top if k == 1 else bottom), toward, (1 if k == 1 else 2)
        src = s["Gg"].at[L, half, cols(768, col)]
        dst = s["Wg"].at[1, half, pl.ds(768 * slot, 768)]
        return cp(("gx", L, step, k), src, dst, at(dx=k))

    def gz(L, k):
        src = s["Gg"].at[L, rows(144, lax.rem(z + k, 4)), cols(768, x)]
        dst = s["Wg"].at[1, pl.ds(144 * (k - 1), 144), pl.ds(2304, 768)]
        return cp(("gz", L, k), src, dst, at(dz=k))

    def y_target(L, k):
        yy = lax.rem(y + k, 4)
        return lax.div(yy, 2) == L, lax.rem(yy, 2)

    def gy(L, k):
        _, ours = y_target(L, k)
        return cp(("gy", L, k), s["Sg"].at[2 * L + ours], s["Yg"].at[k - 1], at(dy=k))

    def gfx(L, k):
        return cp(("gfx", L, k), s["Xg"].at[x], s["Xg"].at[x], at(dx=k))

    def gfs(L, k):
        part = s["Xg"].at[lax.rem(x + 4 - k, 4)]
        return cp(("gfs", L, k), part, part, at(dc=1))

    def og_put():
        for i in range(4):
            s["VG"][:, 768 * i : 768 * i + 768] = s["Xg"][i].astype(F32)
        store["g"].start()

    def put(m):
        if m != "q":
            store[m].start()
            return
        every = s["VQ"][...]
        s["VQ2"][...] = every[:, 192:768]
        s["VKV"][...] = jnp.concatenate([every[:, :192], every[:, 768:960]], axis=1)
        eye = lax.broadcasted_iota(jnp.int32, (72, 72), 0) == lax.broadcasted_iota(jnp.int32, (72, 72), 1)
        s["VGA"][...] = jnp.sum(jnp.where(eye, every[:, 960:961], 0.0), axis=0, keepdims=True)
        s["VGF"][...] = jnp.sum(jnp.where(eye, every[:, 961:962], 0.0), axis=0, keepdims=True)
        for each in ("q", "kv", "ga", "gf"):
            store[each].start()

    def give(i, **way):
        for k in (1, 2, 3):
            where = at(**{axis: k for axis in way})
            pl.semaphore_signal(free.at[i], inc=1, device_id=where, device_id_type=MESH)

    def a0(L):
        @pl.when(is0)
        def _():
            add_sib("g", L)

    def a1(L):
        @pl.when(is0)
        def _():
            pl.semaphore_wait(free.at[L], 2)
            for k in (1, 3):
                gx(L, 0, k).start()

    def a1b(L):
        @pl.when(is0)
        def _():
            for k in (1, 3):
                gx(L, 1, k).start()
            for k in (1, 3):
                half = pl.ds(0 if k == 1 else 288, 288)
                at_cols = cols(768, lax.rem(x + k, 4))
                gx(L, 0, k).wait_recv()
                both = s["Gg"][L, half, at_cols].astype(F32) + s["Wg"][1, half, :768].astype(F32)
                s["Gg"][L, half, at_cols] = both.astype(BF)
                gx(L, 2, k).start()

    def a2(L):
        @pl.when(is0)
        def _():
            for k in (1, 3):
                gx(L, 1, k).wait_recv()
                gx(L, 2, k).wait_recv()

            @pl.loop(0, 4)
            def _(i):
                t = rows(144, i)
                total = s["Gg"][L, t, cols(768, x)].astype(F32)
                for k in (1, 2):
                    total = total + s["Wg"][1, t, 768 * k : 768 * k + 768].astype(F32)
                s["Gg"][L, t, cols(768, x)] = total.astype(BF)

            if L == 1:
                give2(0)
            pl.semaphore_wait(free.at[4 + L], 3)
            for k in (1, 2, 3):
                gz(L, k).start()

    def a3(L):
        @pl.when(is0)
        def _():
            for k in (1, 2, 3):
                gz(L, k).wait_recv()
            total = s["Gg"][L, rows(144, z), cols(768, x)].astype(F32)
            for k in range(3):
                total = total + s["Wg"][1, 144 * k : 144 * k + 144, 2304:].astype(F32)
            s["Sg"][2 * L] = total[:72].astype(BF)
            s["Sg"][2 * L + 1] = total[72:].astype(BF)
            if L == 1:
                give(4, dz=1)
            for k in (1, 2, 3):
                @pl.when(y_target(L, k)[0])
                def _():
                    gy(L, k).start()

    def a4(L):
        @pl.when(is0 & (sec == L))
        def _():
            for k in (1, 2, 3):
                gy(L, k).wait_recv()
            total = s["Sg"][2 * L + ylo].astype(F32)
            for k in range(3):
                total = total + s["Yg"][k].astype(F32)
            s["Xg"][x] = total.astype(BF)
            for k in (1, 2, 3):
                gfx(L, k).start()
            gfs(L, 0).start()

    def a5(L):
        @pl.when(is0 & (sec == L))
        def _():
            for k in (1, 2, 3):
                gfx(L, k).wait_recv()
                gfs(L, k).start()
            og_put()

    def give2(i):
        for k in (1, 3):
            pl.semaphore_signal(free.at[i], inc=1, device_id=at(dx=k), device_id_type=MESH)

    def bz(m, L, k):
        n = ZN[m]
        src = G[m].at[L, rows(n, lax.rem(z + k, 4))]
        dst = rz(m, L).at[pl.ds(n * (k - 1), n)]
        return cp(("bz", m, L, k), src, dst, at(dz=k))

    def by(m, L, k):
        _, half = y_target(L, k)
        return cp(("by", m, L, k), S[m].at[2 * L + half], YR[m].at[k - 1], at(dy=k))

    def bx(m, L, k):
        return cp(("bx", m, L, k), XR[m].at[x], XR[m].at[x], at(dx=k))

    def bf(m, L):
        return cp(("bf", m, L), OUT[m], OUT[m], at(dc=1))

    def hy(L, k, zz):
        _, half = y_target(L, k)
        src = s["Gd"].at[L, rows(192, 2 * zz + half)]
        dst = s["Wg"].at[1, pl.ds(192 * (k - 1), 192), pl.ds(768 * zz, 640)]
        return cp(("hy", L, k, zz), src, dst, at(dy=k))

    def hz(L, k):
        src = s["Gd"].at[L, rows(192, 2 * lax.rem(z + k, 4) + ylo)]
        return cp(("hz", L, k), src, s["Yd"].at[k - 1], at(dz=k))

    def d1(L):
        @pl.when(is1)
        def _():
            add_sib("d", L)
            if L == 1:
                pl.semaphore_wait(free.at[2], 3)
            for k in (1, 2, 3):
                @pl.when(y_target(L, k)[0])
                def _():
                    for zz in range(4):
                        hy(L, k, zz).start()

    def d2(L):
        @pl.when(is1 & (sec == L))
        def _():
            for k in (1, 2, 3):
                for zz in range(4):
                    hy(L, k, zz).wait_recv()
            for zz in range(4):
                t = rows(192, 2 * zz + ylo)
                total = s["Gd"][L, t, :].astype(F32)
                for k in range(3):
                    total = total + s["Wg"][1, 192 * k : 192 * k + 192, 768 * zz : 768 * zz + 640].astype(F32)
                s["Gd"][L, t, :] = total.astype(BF)
            for k in (1, 2, 3):
                hz(L, k).start()

    def d3(L):
        @pl.when(is1 & (sec == L))
        def _():
            for k in (1, 2, 3):
                hz(L, k).wait_recv()
            total = s["Gd"][L, rows(192, d), :].astype(F32)
            for k in range(3):
                total = total + s["Yd"][k].astype(F32)
            s["Xd"][x] = total.astype(BF)
            for k in (1, 2, 3):
                bx("d", L, k).start()

    def b1(m, L):
        @pl.when(is1)
        def _():
            add_sib(m, L)
            for k in (1, 2, 3):
                bz(m, L, k).start()

    def b2(m, L):
        n = ZN[m]

        @pl.when(is1)
        def _():
            for k in (1, 2, 3):
                bz(m, L, k).wait_recv()
            total = G[m][L, rows(n, z), :].astype(F32)
            for k in range(3):
                total = total + rz(m, L)[n * k : n * k + n, :].astype(F32)
            S[m][2 * L] = total[: n // 2].astype(BF)
            S[m][2 * L + 1] = total[n // 2 :].astype(BF)
            for k in (1, 2, 3):
                @pl.when(y_target(L, k)[0])
                def _():
                    by(m, L, k).start()

    def b3(m, L):
        @pl.when(is1 & (sec == L))
        def _():
            for k in (1, 2, 3):
                by(m, L, k).wait_recv()
            total = S[m][2 * L + ylo].astype(F32)
            for k in range(3):
                total = total + YR[m][k].astype(F32)
            XR[m][x] = total.astype(BF)
            for k in (1, 2, 3):
                bx(m, L, k).start()

    def b4(m, L):
        @pl.when(is1 & (sec == L))
        def _():
            for k in (1, 2, 3):
                bx(m, L, k).wait_recv()
            total = XR[m][0].astype(F32)
            for k in range(1, 4):
                total = total + XR[m][k].astype(F32)
            OUT[m][...] = total[:, : OUT[m].shape[1]]
            bf(m, L).start()
            put(m)

    def grads_done():
        for L in (0, 1):
            @pl.when(is0)
            def _():
                for i in range(4):
                    g_part("d", L, i).wait_send()
                for m in ("q", "o"):
                    g_sib(m, L).wait_send()
                for k in (1, 3):
                    for step in range(3):
                        gx(L, step, k).wait_send()
                for k in (1, 2, 3):
                    gz(L, k).wait_send()

                    @pl.when(y_target(L, k)[0])
                    def _():
                        gy(L, k).wait_send()

            @pl.when(is1)
            def _():
                for i in range(4):
                    g_part("g", L, i).wait_send()
                for k in (1, 2, 3):
                    @pl.when(y_target(L, k)[0])
                    def _():
                        for zz in range(4):
                            hy(L, k, zz).wait_send()
                for m in ("q", "o"):
                    for k in (1, 2, 3):
                        bz(m, L, k).wait_send()

                        @pl.when(y_target(L, k)[0])
                        def _():
                            by(m, L, k).wait_send()

            @pl.when(is0 & (sec == L))
            def _():
                for k in (1, 2, 3):
                    gfx(L, k).wait_send()
                for k in range(4):
                    gfs(L, k).wait_send()
                for m in ("d", "o", "q"):
                    bf(m, L).wait_recv()
                    put(m)

            @pl.when(is1 & (sec == L))
            def _():
                for k in (1, 2, 3):
                    hz(L, k).wait_send()
                for m in OTHERS:
                    for k in (1, 2, 3):
                        bx(m, L, k).wait_send()
                    bf(m, L).wait_send()
                for k in range(4):
                    gfs(L, k).wait_recv()
                og_put()

    def dkv_up(L):
        return cp(("du", L), s["DKV"], s["DS"], at(dc=1))

    def dkv_x(L, k):
        src = s["DKV"].at[pl.ds(2 * lax.rem(x + k, 4), 2)]
        return cp(("dx", L, k), src, s["DX"].at[L, k - 1], at(dx=k))

    def dkv_down(L):
        return cp(("dd", L), s["SND"], s["TOT"], at(dc=1))

    def backward(L, xin, dF, mid):
        gain_a, gain_f = gains(L)
        dlow = dF.astype(BF)
        if L == 1:
            s["IGB"][...] = dlow

        @pl.loop(0, 4)
        def _(q):
            up = s["IGB"][...]
            gh = mm_nt(up, s["Wd"][L, rows(384, q), :])
            g = s["GU"][L, :, cols(384, q)].astype(F32)
            u = s["GU"][L, :, cols(384, q + 4)].astype(F32)
            sig = 1.0 / (1.0 + jnp.exp(-g))
            s["GU"][L, :, cols(384, q)] = (gh * u * (sig * (1.0 + g * (1.0 - sig)))).astype(BF)
            s["GU"][L, :, cols(384, q + 4)] = (gh * (g * sig)).astype(BF)
            s["Gd"][L, rows(384, q), :D] = mm_tn(s["HID"][L, :, cols(384, q)], up).astype(BF)
            grad_out("d", L, q)

        s["ACC"][...] = jnp.zeros((R, D), F32)

        @pl.loop(0, 4)
        def _(q):
            gg = s["GU"][L, :, cols(768, q)]
            s["Gg"][L, :, cols(768, q)] = mm_tn(s["NF"][L], gg).astype(BF)
            grad_out("g", L, q)
            s["ACC"][...] += mm_nt(gg, s["Wg"][L, :, cols(768, q)])

        if L == 1:
            @pl.when(is0)
            def _():
                give2(1)
                give(5, dz=1)

            @pl.when(is1)
            def _():
                give(2, dy=1)
        gnf = s["ACC"][...]
        mixed = s["MIX"][L]
        r = lax.rsqrt(jnp.mean(mixed * mixed, axis=1, keepdims=True) + EPSILON)
        e = gnf * gain_f
        z_ffn = (gnf * mixed * r).astype(BF)
        gm = dF + r * e - mixed * (r * r * r * jnp.mean(e * mixed, axis=1, keepdims=True))
        gb = gm.astype(BF)
        att = s["ATT"][L]
        s["Go"][L] = mm_tn(att, gb).astype(BF)
        grad_out("o", L)
        ga = mm_nt(gb, s["Wo"][L]).astype(BF)
        mid[0]()
        prod = ga.astype(F32) * att.astype(F32)
        gqs = []
        for kh in range(3):
            keys_h = s["KV"][L, :, 64 * kh : 64 * kh + 64]
            vals_h = s["KV"][L, :, 192 + 64 * kh : 256 + 64 * kh]
            dk = jnp.zeros((64, 1024), F32)
            dv = jnp.zeros((64, 1024), F32)
            for h in range(3 * kh, 3 * kh + 3):
                lanes = slice(64 * h, 64 * h + 64)
                ga_h = ga[:, lanes]
                p = s["PR"][L, h]
                inner = jnp.sum(prod[:, lanes], axis=1, keepdims=True)
                ds = (p.astype(F32) * (mm_nt(ga_h, vals_h) - inner)).astype(BF)
                dv = dv + mm_tn(ga_h, p)
                dk = dk + mm_tn(s["QS"][L, :, lanes], ds)
                gqs.append(mm(ds, keys_h) * 0.125)
            dk, dv = dk.astype(BF), dv.astype(BF)
            for c in range(8):
                s["DKV"][c, 64 * kh : 64 * kh + 64, :] = dk[:, R * c : R * c + R]
                s["DKV"][c, 192 + 64 * kh : 256 + 64 * kh, :] = dv[:, R * c : R * c + R]
        mid[1]()

        @pl.when(is0)
        def _():
            dkv_up(L).start()

        @pl.when(is1)
        def _():
            dkv_up(L).wait_recv()
            s["DKV"][...] = (s["DKV"][...].astype(F32) + s["DS"][...].astype(F32)).astype(BF)
            for k in (1, 2, 3):
                dkv_x(L, k).start()

        mid[2]()

        @pl.when(is1)
        def _():
            total = s["DKV"][pl.ds(2 * x, 2)].astype(F32)
            for k in (1, 2, 3):
                dkv_x(L, k).wait_recv()
                total = total + s["DX"][L, k - 1].astype(F32)
            s["SND"][...] = total[0].astype(BF)
            s["TOT"][...] = total[1].astype(BF)
            dkv_down(L).start()
            for k in (1, 2, 3):
                dkv_x(L, k).wait_send()
            dkv_down(L).wait_send()

        @pl.when(is0)
        def _():
            dkv_down(L).wait_recv()
            dkv_up(L).wait_send()

        mid[3]()
        total = s["TOT"][...].astype(F32)
        gkv = total.T
        kq = jnp.concatenate([gkv[:, :192]] + gqs, axis=1)
        kq = kq * tiled(s["COS"][...], 6) - swap(kq) * tiled(s["SIN"][...], 6)
        gall = jnp.concatenate([kq, gkv[:, 192:], jnp.zeros((R, 64), F32)], axis=1).astype(BF)
        r = lax.rsqrt(jnp.mean(xin * xin, axis=1, keepdims=True) + EPSILON)
        gn = mm_nt(gall, s["Wq"][L])
        z_att = (gn * xin * r).astype(BF)
        sel = lax.broadcasted_iota(jnp.int32, (2 * R, 128), 1) - lax.broadcasted_iota(jnp.int32, (2 * R, 128), 0) // R
        tail = mm_tn(jnp.concatenate([z_att, z_ffn], axis=0), (sel == 64).astype(F32).astype(BF))
        gw = mm_tn(s["NRM"][L], gall)
        s["Gq"][L, :, :896] = gw[:, :896].astype(BF)
        s["Gq"][L, :, 896:] = (gw[:, 896:] + tail).astype(BF)
        grad_out("q", L)
        e = gn * gain_a
        dx = gm + r * e - xin * (r * r * r * jnp.mean(e * xin, axis=1, keepdims=True))
        low = dx.astype(BF)
        return low

    def put_ig(L, low):
        if L == 1:
            s["IGB"][...] = low
        s["IGT1" if L == 1 else "IGT"][...] = low.astype(F32).T.astype(BF)

        @pl.when(sec == L)
        def _():
            store["ig%d" % L].start()

        @pl.when(sec != L)
        def _():
            ig_send(1 if L == 1 else 0).start()

    none = lambda: None
    ag_start_z("g", 0)
    down_send(0)
    ag_start_z("q", 0)
    ag_start_o()
    tables()
    ag_fwd_x(0)
    ag_fwd_sib("q", 0)

    def f00():
        ag_start_z("g", 1)
        ag_start_z("o", 0)
        ag_start_z("q", 1)
        ag_fwd_x2(0)

    def f01():
        ag_start_z("o", 1)

    def f02():
        ag_fwd_sib("o", 0)
        down_have(0)
        down_send(1)

    def f05():
        ag_fwd_x(1)

    def f03():
        ag_fwd_sib_g(0)
        ag_fwd_sib("q", 1)

    load["tok"].wait()
    s["TOK"][...] = s["TOKT"][...].astype(F32).T.astype(BF)
    forward(0, s["TOK"][...].astype(F32), (f00, f01, f02, f03, none, f05))

    def f10():
        ag_fwd_x2(1)

    def f12():
        ag_fwd_sib("o", 1)

    def f13():
        ag_fwd_sib_g(1)
        down_have(1)

    forward(1, s["HSB"][...].astype(F32), (f10, none, f12, f13, none, none))
    ag_done()
    kv_done(0)
    kv_done(1)

    def c11():
        a0(1)
        a1(1)
        d1(1)
        b1("o", 1)

    def c12():
        a1b(1)

    load["cot"].wait()
    low = backward(1, s["HSB"][...].astype(F32), s["COTT"][...].astype(F32).T, (none, c11, c12, none))
    put_ig(1, low)
    b2("o", 1)

    def c00():
        a2(1)
        a0(0)
        a1(0)
        d1(0)
        b1("q", 1)

    def c01():
        b1("o", 0)

    def c02():
        a1b(0)
        d2(1)

    def c03():
        a3(1)
        b2("q", 1)
        b2("o", 0)

    low = backward(0, s["TOK"][...].astype(F32), s["IGB"][...].astype(F32), (c00, c01, c02, c03))
    put_ig(0, low)
    b1("q", 0)
    a2(0)
    a4(1)
    d3(1)
    b3("o", 1)
    b3("q", 1)
    b3("o", 0)
    d2(0)
    b2("q", 0)
    a3(0)
    d3(0)
    b3("q", 0)
    a5(1)
    b4("o", 1)
    b4("q", 1)
    b4("d", 1)
    a4(0)
    b4("o", 0)
    b4("d", 0)
    b4("q", 0)
    a5(0)
    grads_done()

    for m in ("g", "d", "o", "q", "kv", "ga", "gf"):
        store[m].wait()

    @pl.when(sec == 0)
    def _():
        store["hs0"].wait()
        store["ig0"].wait()
        hs_send(1).wait()
        ig_send(1).wait()

    @pl.when(sec == 1)
    def _():
        store["hs1"].wait()
        store["ig1"].wait()
        hs_send(0).wait()
        ig_send(0).wait()


def hand_on(*refs):
    n = 9
    sems = refs[-1]
    into = [pltpu.make_async_copy(refs[i], refs[2 * n + i], sems.at[0, i]) for i in range(n)]
    out = [pltpu.make_async_copy(refs[2 * n + i], refs[n + i], sems.at[1, i]) for i in range(n)]
    for copy in into:
        copy.start()
    for i in range(n):
        into[i].wait()
        out[i].start()
    for copy in out:
        copy.wait()


def body(tokens, cotangent, block_map, gain_a, w_q, w_kv, w_o, gain_f, w_gu, w_d):
    any_ = pl.BlockSpec(memory_space=pl.ANY)
    vm = pl.BlockSpec(memory_space=pltpu.VMEM)
    shapes = (
        jax.ShapeDtypeStruct((1, 2, D, R), BF),
        jax.ShapeDtypeStruct((1, 2, D, R), BF),
        jax.ShapeDtypeStruct((1, 72), F32),
        jax.ShapeDtypeStruct((1, 72, D), F32),
        jax.ShapeDtypeStruct((1, 72, 384), F32),
        jax.ShapeDtypeStruct((1, 72, D), F32),
        jax.ShapeDtypeStruct((1, 72), F32),
        jax.ShapeDtypeStruct((1, 72, 2 * FF), F32),
        jax.ShapeDtypeStruct((1, 192, D), F32),
    )
    outs = pl.pallas_call(
        mega,
        out_shape=shapes,
        in_specs=[any_, any_, pl.BlockSpec(memory_space=pltpu.SMEM), vm, vm] + [any_] * 5,
        out_specs=(any_,) * 9,
        scratch_shapes=[pltpu.VMEM(shape, dtype) for shape, dtype in SCRATCH.values()]
        + [pltpu.SemaphoreType.DMA((N_SEMS,))] * 2
        + [pltpu.SemaphoreType.REGULAR((6,)), pltpu.SemaphoreType.DMA((16,))],
        compiler_params=pltpu.CompilerParams(
            collective_id=0, has_side_effects=True, vmem_limit_bytes=64 * 2**20
        ),
        name="layers",
    )(tokens.swapaxes(1, 2), cotangent.swapaxes(1, 2), block_map, gain_a, gain_f, w_q, w_kv, w_o, w_gu, w_d)
    hs, ig, *grads = pl.pallas_call(
        hand_on,
        out_shape=shapes,
        in_specs=[any_] * 9,
        out_specs=(any_,) * 9,
        scratch_shapes=[pltpu.VMEM(a.shape, a.dtype) for a in shapes] + [pltpu.SemaphoreType.DMA((2, 9))],
        name="results",
    )(*outs)
    return (hs.swapaxes(2, 3), ig.swapaxes(2, 3), *grads)


def solution(mesh):
    torus = Mesh(mesh.devices.reshape(2, 4, 2, 4, 2), ("section", "z", "ylo", "x", "core"))
    return jax.shard_map(
        body,
        mesh=torus,
        in_specs=(
            P(DP, CONTEXT, None),
            P(DP, CONTEXT, None),
            P(DP, None),
            P("section", DP),
            P("section", DP, None),
            P("section", DP, None),
            P("section", DP, None),
            P("section", DP),
            P("section", DP, None),
            P("section", DP, None),
        ),
        out_specs=(
            P("section", DP, CONTEXT, None),
            P("section", DP, CONTEXT, None),
            P("section", DP),
            P("section", DP, None),
            P("section", DP, None),
            P("section", DP, None),
            P("section", DP),
            P("section", DP, None),
            P("section", DP, None),
        ),
        check_vma=False,
    )
```

```python
import jax
import jax.numpy as jnp
from jax import lax
from jax.experimental import pallas as pl
from jax.experimental.pallas import tpu as pltpu
from jax.sharding import Mesh
from jax.sharding import PartitionSpec as P

CONTEXT = ("x", "core")
DP = ("z", "ylo")
EPSILON = 1e-05
ROPE_BASE = 100000.0
BF = jnp.bfloat16
F32 = jnp.float32
R = 128
D = 576
FF = 1536
MESH = pl.DeviceIdType.MESH

NT = (((1,), (1,)), ((), ()))
TN = (((0,), (0,)), ((), ()))


def mm(a, b):
    return jnp.dot(a, b, preferred_element_type=F32)


def mm_nt(a, b):
    return lax.dot_general(a, b, NT, preferred_element_type=F32)


def mm_tn(a, b):
    return lax.dot_general(a, b, TN, preferred_element_type=F32)


SCRATCH = dict(
    Wg=((2, D, 2 * FF), BF),
    Wq=((2, D, 1024), BF),
    Wo=((2, D, D), BF),
    Wd=((2, FF, D), BF),
    Gg=((2, D, 2 * FF), BF),
    Gq=((2, D, 1024), BF),
    Go=((2, D, D), BF),
    Gd=((2, FF, 640), BF),
    Rg=((D, 2 * FF), BF),
    Rq=((D, 1024), BF),
    Ro=((D, D), BF),
    Rd=((FF, 640), BF),
    Sg=((4, 72, 768), BF),
    Sq=((4, 72, 1024), BF),
    So=((4, 72, D), BF),
    Yg=((3, 72, 768), BF),
    Yq=((3, 72, 1024), BF),
    Yo=((3, 72, D), BF),
    Yd=((3, 192, 640), BF),
    Xq=((4, 72, 1024), BF),
    Xo=((4, 72, D), BF),
    Xd=((4, 192, 640), BF),
    Xg=((4, 72, 768), BF),
    PR=((2, 9, R, 1024), BF),
    GU=((2, R, 2 * FF), BF),
    KV=((2, 1024, 384), BF),
    HID=((2, R, FF), BF),
    NRM=((2, R, D), BF),
    NF=((2, R, D), BF),
    ATT=((2, R, D), BF),
    QS=((2, R, D), BF),
    MIX=((2, R, D), F32),
    HSB=((R, D), BF),
    IGB=((R, D), BF),
    ACC=((R, D), F32),
    DKV=((8, 384, R), BF),
    DS=((8, 384, R), BF),
    DX=((2, 3, 2, 384, R), BF),
    SND=((384, R), BF),
    TOT=((384, R), BF),
    GN=((2, 8, D), F32),
    COS=((R, R), F32),
    SIN=((R, R), F32),
    BIAS=((R, 1024), F32),
    TOK=((R, D), BF),
    TOKT=((D, R), BF),
    COTT=((D, R), BF),
    HST=((D, R), BF),
    HST1=((D, R), BF),
    IGT=((D, R), BF),
    IGT1=((D, R), BF),
    IQ=((72, D), BF),
    IKV=((72, 384), BF),
    VG=((72, 2 * FF), F32),
    VD=((192, D), F32),
    VO=((72, D), F32),
    VQ=((72, 1024), F32),
    VQ2=((72, D), F32),
    VKV=((72, 384), F32),
    VGA=((1, 72), F32),
    VGF=((1, 72), F32),
)
N_SEMS = 256


def mega(tok, cot, bm, gain_a, gain_f, wq, wkv, wo, wg, wd, hs, ig, o_ga, o_q, o_kv, o_o, o_gf, o_g, o_d, *scratch):
    s = dict(zip(SCRATCH, scratch))
    ss, rs, free, ls = scratch[-4:]
    sec = lax.axis_index("section")
    z = lax.axis_index("z")
    ylo = lax.axis_index("ylo")
    x = lax.axis_index("x")
    core = lax.axis_index("core")
    y = sec * 2 + ylo
    d = z * 2 + ylo
    ctx = x * 2 + core
    is0, is1 = core == 0, core == 1

    keys = {}

    def sem(key):
        if key not in keys:
            keys[key] = len(keys)
            assert len(keys) <= N_SEMS
        return keys[key]

    def at(dy=0, dz=0, dx=0, dc=0):
        yy = lax.rem(y + dy, 4)
        return (
            lax.div(yy, 2),
            lax.rem(z + dz, 4),
            lax.rem(yy, 2),
            lax.rem(x + dx, 4),
            lax.rem(core + dc, 2),
        )

    def cp(key, src, dst, where):
        i = sem(key)
        return pltpu.make_async_remote_copy(
            src_ref=src,
            dst_ref=dst,
            send_sem=ss.at[i],
            recv_sem=rs.at[i],
            device_id=where,
            device_id_type=MESH,
        )

    def rows(n, i):
        return pl.ds(pl.multiple_of(n * i, 16), n)

    def cols(n, i):
        return pl.ds(pl.multiple_of(n * i, 128), n)

    def here(i, src, dst):
        return pltpu.make_async_copy(src, dst, ls.at[i])

    load = dict(
        tok=here(0, tok.at[sec], s["TOKT"]),
        cot=here(1, cot.at[sec], s["COTT"]),
        q=here(2, wq.at[0], s["IQ"]),
        kv=here(3, wkv.at[0], s["IKV"]),
        o=here(4, wo.at[0], s["So"].at[y]),
        d=here(5, wd.at[0], s["Wd"].at[sec, rows(192, d)]),
        g=here(6, wg.at[0, :, cols(768, x)], s["Sg"].at[y]),
    )
    store = dict(
        g=here(7, s["VG"], o_g.at[0]),
        d=here(8, s["VD"], o_d.at[0]),
        o=here(9, s["VO"], o_o.at[0]),
        q=here(10, s["VQ2"], o_q.at[0]),
        kv=here(11, s["VKV"], o_kv.at[0]),
        ga=here(12, s["VGA"], o_ga),
        gf=here(13, s["VGF"], o_gf),
        hs0=here(14, s["HST"], hs.at[0, sec]),
        hs1=here(14, s["HST1"], hs.at[0, sec]),
        ig0=here(15, s["IGT"], ig.at[0, sec]),
        ig1=here(15, s["IGT1"], ig.at[0, sec]),
    )

    load["tok"].start()

    @pl.when(is1)
    def _():
        for m in ("q", "kv", "d", "o"):
            load[m].start()

    @pl.when(is0)
    def _():
        load["g"].start()

    load["cot"].start()

    barrier = pltpu.get_barrier_semaphore()
    peers = [at(dy=k) for k in (1, 2, 3)] + [at(dz=k) for k in (1, 2, 3)]
    peers += [at(dx=k) for k in (1, 2, 3)] + [at(dc=1)]
    for p in peers:
        pl.semaphore_signal(barrier, inc=1, device_id=p, device_id_type=MESH)
    pl.semaphore_wait(barrier, len(peers))

    W = dict(q=s["Wq"], o=s["Wo"], d=s["Wd"])
    S = dict(q=s["Sq"], o=s["So"])
    own = dict(q=s["Sq"].at[y], o=wo.at[0])
    OTHERS = ("q", "o", "d")

    def ag_y(m, k):
        if m == "g":
            return cp(("ay", m, k), wg.at[0, :, cols(768, x)], s["Sg"].at[y], at(dy=k))
        return cp(("ay", m, k), own[m], S[m].at[y], at(dy=k))

    def down_z(k):
        return cp(("dz", k), wd.at[0], s["Wd"].at[sec, rows(192, d)], at(dz=k))

    def down_y(k, zz):
        part = s["Wd"].at[sec, rows(192, 2 * zz + ylo)]
        return cp(("dy", k, zz), part, part, at(dy=k))

    def from_section(k):
        return lax.div(lax.rem(y + 4 - k, 4), 2)

    def ag_z(m, L, k):
        if m == "g":
            part = s["Wg"].at[L, rows(144, z), cols(768, x)]
        else:
            part = W[m].at[L, rows(144, z)]
        return cp(("az", m, L, k), part, part, at(dz=k))

    def ag_x(L, k):
        part = s["Wg"].at[L, :, cols(768, x)]
        return cp(("ax", L, k), part, part, at(dx=k))

    def ag_x2(L, k):
        part = s["Wg"].at[L, pl.ds(0 if k == 1 else 288, 288), cols(768, lax.rem(x + 4 - k, 4))]
        return cp(("ax2", L, k), part, part, at(dx=k))

    def ag_sib_g(L, k):
        part = s["Wg"].at[L, :, cols(768, lax.rem(x + 4 - k, 4))]
        return cp(("asg", L, k), part, part, at(dc=1))

    def ag_sib(m, L):
        part = W[m].at[L]
        return cp(("as", m, L), part, part, at(dc=1))

    def join(m, L):
        buf = s["Sg"] if m == "g" else S[m]
        both = jnp.concatenate([buf[2 * L + h].astype(F32) for h in (0, 1)], axis=0).astype(BF)
        if m == "g":
            s["Wg"][L, rows(144, z), cols(768, x)] = both
        else:
            W[m][L, rows(144, z), :] = both

    @pl.when(is0)
    def _():
        for k in (2, 1, 3):
            ag_y("g", k).start()
        load["g"].wait()

    @pl.when(is1)
    def _():
        eye = lax.broadcasted_iota(jnp.int32, (72, 72), 0) == lax.broadcasted_iota(jnp.int32, (72, 72), 1)
        gain = [jnp.sum(jnp.where(eye, g[...].astype(F32), 0.0), axis=1, keepdims=True) for g in (gain_a, gain_f)]
        load["q"].wait()
        load["kv"].wait()
        kv = s["IKV"][...].astype(F32)
        parts = [kv[:, :192], s["IQ"][...].astype(F32), kv[:, 192:], *gain, jnp.zeros((72, 62), F32)]
        s["Sq"][y] = jnp.concatenate(parts, axis=1).astype(BF)
        for k in (2, 1, 3):
            ag_y("q", k).start()
        for k in (2, 1, 3):
            down_z(k).start()
        load["d"].wait()
        load["o"].wait()

    def tables():
        lane = lax.broadcasted_iota(jnp.int32, (R, R), 1)
        row = lax.broadcasted_iota(jnp.int32, (R, R), 0)
        first = row < 64
        pos_t = jnp.where(first, bm[sec, 2 * ctx], bm[sec, 2 * ctx + 1]) * 64 + jnp.where(first, row, row - 64)
        freq = jnp.exp((lane % 32).astype(F32) * F32(-2.0 / 64 * jnp.log(ROPE_BASE)))
        angle = pos_t.astype(F32) * freq
        s["COS"][...] = jnp.cos(angle)
        sine = jnp.sin(angle)
        s["SIN"][...] = jnp.where(lane % 64 < 32, -sine, sine)
        pos_f = pos_t[:, :1].astype(F32)
        for j in range(16):
            u = lax.broadcasted_iota(jnp.int32, (R, 64), 1) + bm[sec, j] * 64
            s["BIAS"][:, 64 * j : 64 * j + 64] = jnp.where(u.astype(F32) <= pos_f, 0.0, -1e30).astype(F32)

    def ag_start_o():
        @pl.when(is1)
        def _():
            for k in (2, 1, 3):
                ag_y("o", k).start()

    def wait_y(m):
        for k in (1, 2, 3):
            ag_y(m, k).wait_recv()

    def ag_start_z(m, L):
        @pl.when(is0 if m == "g" else is1)
        def _():
            if L == 0:
                wait_y(m)
            join(m, L)
            for k in (2, 1, 3):
                ag_z(m, L, k).start()

    def down_send(L):
        @pl.when(is1 & (sec == L))
        def _():
            for k in (1, 2, 3):
                down_z(k).wait_recv()
            for zz in range(4):
                for k in (2, 1, 3):
                    down_y(k, zz).start()

    def down_have(L):
        @pl.when(is1)
        def _():
            for k in (1, 2, 3):
                @pl.when(from_section(k) == L)
                def _():
                    for zz in range(4):
                        down_y(k, zz).wait_recv()
            ag_sib("d", L).start()

    def ag_fwd_x(L):
        @pl.when(is0)
        def _():
            for k in (1, 2, 3):
                ag_z("g", L, k).wait_recv()
            for k in (1, 3):
                ag_x(L, k).start()
            ag_sib_g(L, 0).start()

    def ag_fwd_x2(L):
        @pl.when(is0)
        def _():
            for k in (1, 3):
                ag_x(L, k).wait_recv()
                ag_x2(L, k).start()
            for k in (1, 3):
                ag_sib_g(L, k).start()

    def ag_fwd_sib(m, L):
        @pl.when(is1)
        def _():
            for k in (1, 2, 3):
                ag_z(m, L, k).wait_recv()
            ag_sib(m, L).start()

    def ag_fwd_sib_g(L):
        @pl.when(is0)
        def _():
            for k in (1, 3):
                ag_x2(L, k).wait_recv()
            ag_sib_g(L, 2).start()

    def need(m, L):
        if m == "g":
            @pl.when(is1)
            def _():
                for k in (0, 1, 2, 3):
                    ag_sib_g(L, k).wait_recv()
        else:
            @pl.when(is0)
            def _():
                ag_sib(m, L).wait_recv()

    def ag_done():
        @pl.when(is1)
        def _():
            for k in (1, 2, 3):
                down_z(k).wait_send()
                for zz in range(4):
                    down_y(k, zz).wait_send()
            for m in OTHERS:
                if m != "d":
                    for k in (1, 2, 3):
                        ag_y(m, k).wait_send()
                for L in (0, 1):
                    if m != "d":
                        for k in (1, 2, 3):
                            ag_z(m, L, k).wait_send()
                    ag_sib(m, L).wait_send()

        @pl.when(is0)
        def _():
            for k in (1, 2, 3):
                ag_y("g", k).wait_send()
            for L in (0, 1):
                for k in (1, 2, 3):
                    ag_z("g", L, k).wait_send()
                for k in (1, 3):
                    ag_x(L, k).wait_send()
                    ag_x2(L, k).wait_send()
                for k in (0, 1, 2, 3):
                    ag_sib_g(L, k).wait_send()

    def tiled(t, n):
        return jnp.concatenate([t] * n, axis=1)

    def swap(v):
        width = v.shape[1]
        ahead = pltpu.roll(v, width - 32, 1)
        behind = pltpu.roll(v, 32, 1)
        low = lax.broadcasted_iota(jnp.int32, v.shape, 1) % 64 < 32
        return jnp.where(low, ahead, behind)

    def gains(L):
        eye = (
            lax.broadcasted_iota(jnp.int32, (D, D), 0) == lax.broadcasted_iota(jnp.int32, (D, D), 1)
        ).astype(F32).astype(BF)
        both = mm_tn(s["Wq"][L, :, 896:1024], eye)
        s["GN"][L] = both[64:72]
        return both[64:65], both[65:66]

    def kv_up(L):
        part = s["KV"].at[L, rows(R, ctx)]
        return cp(("ku", L), part, part, at(dc=1))

    def kv_x(L, who, k):
        part = s["KV"].at[L, rows(R, 2 * x + who)]
        return cp(("kx", L, who, k), part, part, at(dx=k))

    def kv_down(L, k):
        part = s["KV"].at[L, rows(2 * R, lax.rem(x + 4 - k, 4))]
        return cp(("kd", L, k), part, part, at(dc=1))

    def kv_done(L):
        kv_up(L).wait_send()

        @pl.when(is1)
        def _():
            for k in (1, 2, 3):
                for who in (0, 1):
                    kv_x(L, who, k).wait_send()
                kv_down(L, k).wait_send()

    def hs_send(L):
        return cp("hs", s["HST1" if L == 1 else "HST"], hs.at[0, sec], at(dy=2))

    def ig_send(L):
        return cp("ig", s["IGT1" if L == 1 else "IGT"], ig.at[0, sec], at(dy=2))

    def forward(L, xin, mid):
        need("q", L)
        gain_a, gain_f = gains(L)
        r = lax.rsqrt(jnp.mean(xin * xin, axis=1, keepdims=True) + EPSILON)
        normed = (xin * r * gain_a).astype(BF)
        s["NRM"][L] = normed
        qkv = mm(normed, s["Wq"][L])
        kq = qkv[:, :768]
        kq = kq * tiled(s["COS"][...], 6) + swap(kq) * tiled(s["SIN"][...], 6)
        s["KV"][L, rows(R, ctx), :] = jnp.concatenate([kq[:, :192], qkv[:, 768:960]], axis=1).astype(BF)
        kv_up(L).start()

        @pl.when(is1)
        def _():
            for k in (1, 2, 3):
                kv_x(L, 1, k).start()
            kv_up(L).wait_recv()
            for k in (2, 1, 3):
                kv_x(L, 0, k).start()

        s["QS"][L] = (kq[:, 192:768] * 0.125).astype(BF)
        mid[0]()

        @pl.when(is1)
        def _():
            for k in (1, 2, 3):
                for who in (0, 1):
                    kv_x(L, who, k).wait_recv()
                kv_down(L, k).start()

        mid[1]()

        @pl.when(is0)
        def _():
            kv_up(L).wait_recv()
            for k in (1, 2, 3):
                kv_down(L, k).wait_recv()

        mid[5]()
        outs = []
        for kh in range(3):
            keys_h = s["KV"][L, :, 64 * kh : 64 * kh + 64]
            vals_h = s["KV"][L, :, 192 + 64 * kh : 256 + 64 * kh]
            for h in range(3 * kh, 3 * kh + 3):
                sc = mm_nt(s["QS"][L, :, 64 * h : 64 * h + 64], keys_h) + s["BIAS"][...]
                e = jnp.exp(sc - jnp.max(sc, axis=1, keepdims=True))
                p = (e * (1.0 / jnp.sum(e, axis=1, keepdims=True))).astype(BF)
                s["PR"][L, h] = p
                outs.append(mm(p, vals_h))
        att = jnp.concatenate(outs, axis=1).astype(BF)
        s["ATT"][L] = att
        mid[2]()
        need("o", L)
        mixed = xin + mm(att, s["Wo"][L])
        s["MIX"][L] = mixed
        r = lax.rsqrt(jnp.mean(mixed * mixed, axis=1, keepdims=True) + EPSILON)
        s["NF"][L] = (mixed * r * gain_f).astype(BF)
        mid[3]()
        need("g", L)

        @pl.loop(0, 4)
        def _(q):
            nf = s["NF"][L]
            g = mm(nf, s["Wg"][L, :, cols(384, q)])
            u = mm(nf, s["Wg"][L, :, cols(384, q + 4)])
            s["GU"][L, :, cols(384, q)] = g.astype(BF)
            s["GU"][L, :, cols(384, q + 4)] = u.astype(BF)
            s["HID"][L, :, cols(384, q)] = (g / (1.0 + jnp.exp(-g)) * u).astype(BF)

        mid[4]()
        need("d", L)
        out = (s["MIX"][L] + mm(s["HID"][L], s["Wd"][L])).astype(BF)
        if L == 0:
            s["HSB"][...] = out
        s["HST1" if L == 1 else "HST"][...] = out.astype(F32).T.astype(BF)

        @pl.when(sec == L)
        def _():
            store["hs%d" % L].start()

        @pl.when(sec != L)
        def _():
            hs_send(L).start()

    G = dict(q=s["Gq"], o=s["Go"], d=s["Gd"], g=s["Gg"])
    RAW = dict(q=s["Rq"], o=s["Ro"], d=s["Rd"], g=s["Rg"])
    WALL = dict(W, g=s["Wg"])
    ZN = dict(q=144, o=144, d=384)
    YR = dict(q=s["Yq"], o=s["Yo"])
    XR = dict(q=s["Xq"], o=s["Xo"], d=s["Xd"])
    OUT = dict(q=s["VQ"], o=s["VO"], d=s["VD"])

    def ra(m, L):
        return RAW[m] if L == 1 or m in "gd" else WALL[m].at[1]

    def rz(m, L):
        return G[m].at[0] if L == 1 else RAW[m]

    def g_sib(m, L):
        return cp(("gs", m, L), G[m].at[L], ra(m, L), at(dc=1))

    parts = {(m, L): [sem(("part", m, L, i)) for i in range(4)][0] for m in "gd" for L in (0, 1)}

    def g_part(m, L, i):
        at_i = (slice(None), cols(768, i)) if m == "g" else (rows(384, i),)
        j = parts[m, L] + i
        return pltpu.make_async_remote_copy(
            src_ref=G[m].at[(L, *at_i)],
            dst_ref=ra(m, L).at[at_i],
            send_sem=ss.at[j],
            recv_sem=rs.at[j],
            device_id=at(dc=1),
            device_id_type=MESH,
        )

    def grad_out(m, L, i=None):
        @pl.when(is1 if m == "g" else is0)
        def _():
            (g_sib(m, L) if i is None else g_part(m, L, i)).start()

    def add_sib(m, L):
        if m not in "gd":
            g_sib(m, L).wait_recv()
        ref, other = G[m].at[L], ra(m, L)

        @pl.loop(0, 4)
        def _(i):
            if m in "gd":
                g_part(m, L, i).wait_recv()
            t = (slice(None), cols(768, i)) if m == "g" else (rows(ref.shape[0] // 4, i), slice(None))
            ref[t] = (ref[t].astype(F32) + other[t].astype(F32)).astype(BF)

    def gx(L, step, k):
        toward = lax.rem(x + k, 4)
        top = pl.ds(0, 288)
        bottom = pl.ds(288, 288)
        if step == 0:
            half, col, slot = (top if k == 1 else bottom), lax.rem(x + 2, 4), 0
        elif step == 1:
            half, col, slot = (bottom if k == 1 else top), toward, (1 if k == 1 else 2)
        else:
            half, col, slot = (top if k == 1 else bottom), toward, (1 if k == 1 else 2)
        src = s["Gg"].at[L, half, cols(768, col)]
        dst = s["Wg"].at[1, half, pl.ds(768 * slot, 768)]
        return cp(("gx", L, step, k), src, dst, at(dx=k))

    def gz(L, k):
        src = s["Gg"].at[L, rows(144, lax.rem(z + k, 4)), cols(768, x)]
        dst = s["Wg"].at[1, pl.ds(144 * (k - 1), 144), pl.ds(2304, 768)]
        return cp(("gz", L, k), src, dst, at(dz=k))

    def y_target(L, k):
        yy = lax.rem(y + k, 4)
        return lax.div(yy, 2) == L, lax.rem(yy, 2)

    def gy(L, k):
        _, ours = y_target(L, k)
        return cp(("gy", L, k), s["Sg"].at[2 * L + ours], s["Yg"].at[k - 1], at(dy=k))

    def gfx(L, k):
        return cp(("gfx", L, k), s["Xg"].at[x], s["Xg"].at[x], at(dx=k))

    def gfs(L, k):
        part = s["Xg"].at[lax.rem(x + 4 - k, 4)]
        return cp(("gfs", L, k), part, part, at(dc=1))

    def og_put():
        for i in range(4):
            s["VG"][:, 768 * i : 768 * i + 768] = s["Xg"][i].astype(F32)
        store["g"].start()

    def put(m):
        if m != "q":
            store[m].start()
            return
        every = s["VQ"][...]
        s["VQ2"][...] = every[:, 192:768]
        s["VKV"][...] = jnp.concatenate([every[:, :192], every[:, 768:960]], axis=1)
        eye = lax.broadcasted_iota(jnp.int32, (72, 72), 0) == lax.broadcasted_iota(jnp.int32, (72, 72), 1)
        s["VGA"][...] = jnp.sum(jnp.where(eye, every[:, 960:961], 0.0), axis=0, keepdims=True)
        s["VGF"][...] = jnp.sum(jnp.where(eye, every[:, 961:962], 0.0), axis=0, keepdims=True)
        for each in ("q", "kv", "ga", "gf"):
            store[each].start()

    def give(i, **way):
        for k in (1, 2, 3):
            where = at(**{axis: k for axis in way})
            pl.semaphore_signal(free.at[i], inc=1, device_id=where, device_id_type=MESH)

    def a0(L):
        @pl.when(is0)
        def _():
            add_sib("g", L)

    def a1(L):
        @pl.when(is0)
        def _():
            pl.semaphore_wait(free.at[L], 2)
            for k in (1, 3):
                gx(L, 0, k).start()

    def a1b(L):
        @pl.when(is0)
        def _():
            for k in (1, 3):
                gx(L, 1, k).start()
            for k in (1, 3):
                half = pl.ds(0 if k == 1 else 288, 288)
                at_cols = cols(768, lax.rem(x + k, 4))
                gx(L, 0, k).wait_recv()
                both = s["Gg"][L, half, at_cols].astype(F32) + s["Wg"][1, half, :768].astype(F32)
                s["Gg"][L, half, at_cols] = both.astype(BF)
                gx(L, 2, k).start()

    def a2(L):
        @pl.when(is0)
        def _():
            for k in (1, 3):
                gx(L, 1, k).wait_recv()
                gx(L, 2, k).wait_recv()

            @pl.loop(0, 4)
            def _(i):
                t = rows(144, i)
                total = s["Gg"][L, t, cols(768, x)].astype(F32)
                for k in (1, 2):
                    total = total + s["Wg"][1, t, 768 * k : 768 * k + 768].astype(F32)
                s["Gg"][L, t, cols(768, x)] = total.astype(BF)

            if L == 1:
                give2(0)
            pl.semaphore_wait(free.at[4 + L], 3)
            for k in (2, 1, 3):
                gz(L, k).start()

    def a3(L):
        @pl.when(is0)
        def _():
            for k in (1, 2, 3):
                gz(L, k).wait_recv()
            total = s["Gg"][L, rows(144, z), cols(768, x)].astype(F32)
            for k in range(3):
                total = total + s["Wg"][1, 144 * k : 144 * k + 144, 2304:].astype(F32)
            s["Sg"][2 * L] = total[:72].astype(BF)
            s["Sg"][2 * L + 1] = total[72:].astype(BF)
            if L == 1:
                give(4, dz=1)
            for k in (2, 1, 3):
                @pl.when(y_target(L, k)[0])
                def _():
                    gy(L, k).start()

    def a4(L):
        @pl.when(is0 & (sec == L))
        def _():
            for k in (1, 2, 3):
                gy(L, k).wait_recv()
            total = s["Sg"][2 * L + ylo].astype(F32)
            for k in range(3):
                total = total + s["Yg"][k].astype(F32)
            s["Xg"][x] = total.astype(BF)
            for k in (2, 1, 3):
                gfx(L, k).start()
            gfs(L, 0).start()

    def a5(L):
        @pl.when(is0 & (sec == L))
        def _():
            for k in (1, 2, 3):
                gfx(L, k).wait_recv()
                gfs(L, k).start()
            og_put()

    def give2(i):
        for k in (1, 3):
            pl.semaphore_signal(free.at[i], inc=1, device_id=at(dx=k), device_id_type=MESH)

    def bz(m, L, k):
        n = ZN[m]
        src = G[m].at[L, rows(n, lax.rem(z + k, 4))]
        dst = rz(m, L).at[pl.ds(n * (k - 1), n)]
        return cp(("bz", m, L, k), src, dst, at(dz=k))

    def by(m, L, k):
        _, half = y_target(L, k)
        return cp(("by", m, L, k), S[m].at[2 * L + half], YR[m].at[k - 1], at(dy=k))

    def bx(m, L, k):
        return cp(("bx", m, L, k), XR[m].at[x], XR[m].at[x], at(dx=k))

    def bf(m, L):
        return cp(("bf", m, L), OUT[m], OUT[m], at(dc=1))

    def hy(L, k, zz):
        _, half = y_target(L, k)
        src = s["Gd"].at[L, rows(192, 2 * zz + half)]
        dst = s["Wg"].at[1, pl.ds(192 * (k - 1), 192), pl.ds(768 * zz, 640)]
        return cp(("hy", L, k, zz), src, dst, at(dy=k))

    def hz(L, k):
        src = s["Gd"].at[L, rows(192, 2 * lax.rem(z + k, 4) + ylo)]
        return cp(("hz", L, k), src, s["Yd"].at[k - 1], at(dz=k))

    def d1(L):
        @pl.when(is1)
        def _():
            add_sib("d", L)
            if L == 1:
                pl.semaphore_wait(free.at[2], 3)
            for k in (1, 2, 3):
                @pl.when(y_target(L, k)[0])
                def _():
                    for zz in range(4):
                        hy(L, k, zz).start()

    def d2(L):
        @pl.when(is1 & (sec == L))
        def _():
            for k in (1, 2, 3):
                for zz in range(4):
                    hy(L, k, zz).wait_recv()
            for zz in range(4):
                t = rows(192, 2 * zz + ylo)
                total = s["Gd"][L, t, :].astype(F32)
                for k in range(3):
                    total = total + s["Wg"][1, 192 * k : 192 * k + 192, 768 * zz : 768 * zz + 640].astype(F32)
                s["Gd"][L, t, :] = total.astype(BF)
            for k in (2, 1, 3):
                hz(L, k).start()

    def d3(L):
        @pl.when(is1 & (sec == L))
        def _():
            for k in (1, 2, 3):
                hz(L, k).wait_recv()
            total = s["Gd"][L, rows(192, d), :].astype(F32)
            for k in range(3):
                total = total + s["Yd"][k].astype(F32)
            s["Xd"][x] = total.astype(BF)
            for k in (2, 1, 3):
                bx("d", L, k).start()

    def b1(m, L):
        @pl.when(is1)
        def _():
            add_sib(m, L)
            for k in (2, 1, 3):
                bz(m, L, k).start()

    def b2(m, L):
        n = ZN[m]

        @pl.when(is1)
        def _():
            for k in (1, 2, 3):
                bz(m, L, k).wait_recv()
            total = G[m][L, rows(n, z), :].astype(F32)
            for k in range(3):
                total = total + rz(m, L)[n * k : n * k + n, :].astype(F32)
            S[m][2 * L] = total[: n // 2].astype(BF)
            S[m][2 * L + 1] = total[n // 2 :].astype(BF)
            for k in (2, 1, 3):
                @pl.when(y_target(L, k)[0])
                def _():
                    by(m, L, k).start()

    def b3(m, L):
        @pl.when(is1 & (sec == L))
        def _():
            for k in (1, 2, 3):
                by(m, L, k).wait_recv()
            total = S[m][2 * L + ylo].astype(F32)
            for k in range(3):
                total = total + YR[m][k].astype(F32)
            XR[m][x] = total.astype(BF)
            for k in (2, 1, 3):
                bx(m, L, k).start()

    def b4(m, L):
        @pl.when(is1 & (sec == L))
        def _():
            for k in (1, 2, 3):
                bx(m, L, k).wait_recv()
            total = XR[m][0].astype(F32)
            for k in range(1, 4):
                total = total + XR[m][k].astype(F32)
            OUT[m][...] = total[:, : OUT[m].shape[1]]
            bf(m, L).start()
            put(m)

    def grads_done():
        for L in (0, 1):
            @pl.when(is0)
            def _():
                for i in range(4):
                    g_part("d", L, i).wait_send()
                for m in ("q", "o"):
                    g_sib(m, L).wait_send()
                for k in (1, 3):
                    for step in range(3):
                        gx(L, step, k).wait_send()
                for k in (1, 2, 3):
                    gz(L, k).wait_send()

                    @pl.when(y_target(L, k)[0])
                    def _():
                        gy(L, k).wait_send()

            @pl.when(is1)
            def _():
                for i in range(4):
                    g_part("g", L, i).wait_send()
                for k in (1, 2, 3):
                    @pl.when(y_target(L, k)[0])
                    def _():
                        for zz in range(4):
                            hy(L, k, zz).wait_send()
                for m in ("q", "o"):
                    for k in (1, 2, 3):
                        bz(m, L, k).wait_send()

                        @pl.when(y_target(L, k)[0])
                        def _():
                            by(m, L, k).wait_send()

            @pl.when(is0 & (sec == L))
            def _():
                for k in (1, 2, 3):
                    gfx(L, k).wait_send()
                for k in range(4):
                    gfs(L, k).wait_send()
                for m in ("d", "o", "q"):
                    bf(m, L).wait_recv()
                    put(m)

            @pl.when(is1 & (sec == L))
            def _():
                for k in (1, 2, 3):
                    hz(L, k).wait_send()
                for m in OTHERS:
                    for k in (1, 2, 3):
                        bx(m, L, k).wait_send()
                    bf(m, L).wait_send()
                for k in range(4):
                    gfs(L, k).wait_recv()
                og_put()

    def dkv_up(L):
        return cp(("du", L), s["DKV"], s["DS"], at(dc=1))

    def dkv_x(L, k):
        src = s["DKV"].at[pl.ds(2 * lax.rem(x + k, 4), 2)]
        return cp(("dx", L, k), src, s["DX"].at[L, k - 1], at(dx=k))

    def dkv_down(L):
        return cp(("dd", L), s["SND"], s["TOT"], at(dc=1))

    def backward(L, xin, dF, mid):
        gain_a, gain_f = s["GN"][L, 0:1, :], s["GN"][L, 1:2, :]
        dlow = dF.astype(BF)
        if L == 1:
            s["IGB"][...] = dlow

        @pl.loop(0, 4)
        def _(q):
            up = s["IGB"][...]
            gh = mm_nt(up, s["Wd"][L, rows(384, q), :])
            g = s["GU"][L, :, cols(384, q)].astype(F32)
            u = s["GU"][L, :, cols(384, q + 4)].astype(F32)
            sig = 1.0 / (1.0 + jnp.exp(-g))
            s["GU"][L, :, cols(384, q)] = (gh * u * (sig * (1.0 + g * (1.0 - sig)))).astype(BF)
            s["GU"][L, :, cols(384, q + 4)] = (gh * (g * sig)).astype(BF)
            s["Gd"][L, rows(384, q), :D] = mm_tn(s["HID"][L, :, cols(384, q)], up).astype(BF)
            grad_out("d", L, q)

        s["ACC"][...] = jnp.zeros((R, D), F32)

        @pl.loop(0, 4)
        def _(q):
            gg = s["GU"][L, :, cols(768, q)]
            s["Gg"][L, :, cols(768, q)] = mm_tn(s["NF"][L], gg).astype(BF)
            grad_out("g", L, q)
            s["ACC"][...] += mm_nt(gg, s["Wg"][L, :, cols(768, q)])

        if L == 1:
            @pl.when(is0)
            def _():
                give2(1)
                give(5, dz=1)

            @pl.when(is1)
            def _():
                give(2, dy=1)
        gnf = s["ACC"][...]
        mixed = s["MIX"][L]
        r = lax.rsqrt(jnp.mean(mixed * mixed, axis=1, keepdims=True) + EPSILON)
        e = gnf * gain_f
        z_ffn = (gnf * mixed * r).astype(BF)
        gm = dF + r * e - mixed * (r * r * r * jnp.mean(e * mixed, axis=1, keepdims=True))
        gb = gm.astype(BF)
        att = s["ATT"][L]
        s["Go"][L] = mm_tn(att, gb).astype(BF)
        grad_out("o", L)
        ga = mm_nt(gb, s["Wo"][L]).astype(BF)
        mid[0]()
        prod = ga.astype(F32) * att.astype(F32)
        gqs = []
        for kh in range(3):
            keys_h = s["KV"][L, :, 64 * kh : 64 * kh + 64]
            vals_h = s["KV"][L, :, 192 + 64 * kh : 256 + 64 * kh]
            dk = jnp.zeros((64, 1024), F32)
            dv = jnp.zeros((64, 1024), F32)
            for h in range(3 * kh, 3 * kh + 3):
                lanes = slice(64 * h, 64 * h + 64)
                ga_h = ga[:, lanes]
                p = s["PR"][L, h]
                inner = jnp.sum(prod[:, lanes], axis=1, keepdims=True)
                ds = (p.astype(F32) * (mm_nt(ga_h, vals_h) - inner)).astype(BF)
                dv = dv + mm_tn(ga_h, p)
                dk = dk + mm_tn(s["QS"][L, :, lanes], ds)
                gqs.append(mm(ds, keys_h) * 0.125)
            dk, dv = dk.astype(BF), dv.astype(BF)
            for c in range(8):
                s["DKV"][c, 64 * kh : 64 * kh + 64, :] = dk[:, R * c : R * c + R]
                s["DKV"][c, 192 + 64 * kh : 256 + 64 * kh, :] = dv[:, R * c : R * c + R]
        mid[1]()

        @pl.when(is0)
        def _():
            dkv_up(L).start()

        @pl.when(is1)
        def _():
            dkv_up(L).wait_recv()
            s["DKV"][...] = (s["DKV"][...].astype(F32) + s["DS"][...].astype(F32)).astype(BF)
            for k in (2, 1, 3):
                dkv_x(L, k).start()

        mid[2]()

        @pl.when(is1)
        def _():
            total = s["DKV"][pl.ds(2 * x, 2)].astype(F32)
            for k in (1, 2, 3):
                dkv_x(L, k).wait_recv()
                total = total + s["DX"][L, k - 1].astype(F32)
            s["SND"][...] = total[0].astype(BF)
            s["TOT"][...] = total[1].astype(BF)
            dkv_down(L).start()
            for k in (1, 2, 3):
                dkv_x(L, k).wait_send()
            dkv_down(L).wait_send()

        @pl.when(is0)
        def _():
            dkv_down(L).wait_recv()
            dkv_up(L).wait_send()

        mid[3]()
        total = s["TOT"][...].astype(F32)
        gkv = total.T
        kq = jnp.concatenate([gkv[:, :192]] + gqs, axis=1)
        kq = kq * tiled(s["COS"][...], 6) - swap(kq) * tiled(s["SIN"][...], 6)
        gall = jnp.concatenate([kq, gkv[:, 192:], jnp.zeros((R, 64), F32)], axis=1).astype(BF)
        r = lax.rsqrt(jnp.mean(xin * xin, axis=1, keepdims=True) + EPSILON)
        gn = mm_nt(gall, s["Wq"][L])
        z_att = (gn * xin * r).astype(BF)
        sel = lax.broadcasted_iota(jnp.int32, (2 * R, 128), 1) - lax.broadcasted_iota(jnp.int32, (2 * R, 128), 0) // R
        tail = mm_tn(jnp.concatenate([z_att, z_ffn], axis=0), (sel == 64).astype(F32).astype(BF))
        gw = mm_tn(s["NRM"][L], gall)
        s["Gq"][L, :, :896] = gw[:, :896].astype(BF)
        s["Gq"][L, :, 896:] = (gw[:, 896:] + tail).astype(BF)
        grad_out("q", L)
        e = gn * gain_a
        dx = gm + r * e - xin * (r * r * r * jnp.mean(e * xin, axis=1, keepdims=True))
        low = dx.astype(BF)
        return low

    def put_ig(L, low):
        if L == 1:
            s["IGB"][...] = low
        s["IGT1" if L == 1 else "IGT"][...] = low.astype(F32).T.astype(BF)

        @pl.when(sec == L)
        def _():
            store["ig%d" % L].start()

        @pl.when(sec != L)
        def _():
            ig_send(1 if L == 1 else 0).start()

    none = lambda: None
    ag_start_z("g", 0)
    down_send(0)
    ag_start_z("q", 0)
    ag_start_o()
    tables()
    ag_fwd_x(0)
    ag_fwd_sib("q", 0)

    def f00():
        ag_start_z("g", 1)
        ag_start_z("o", 0)
        ag_start_z("q", 1)
        ag_fwd_x2(0)

    def f01():
        ag_start_z("o", 1)

    def f02():
        ag_fwd_sib("o", 0)
        down_have(0)
        down_send(1)

    def f05():
        ag_fwd_x(1)

    def f03():
        ag_fwd_sib_g(0)
        ag_fwd_sib("q", 1)

    load["tok"].wait()
    s["TOK"][...] = s["TOKT"][...].astype(F32).T.astype(BF)
    forward(0, s["TOK"][...].astype(F32), (f00, f01, f02, f03, none, f05))

    def f10():
        ag_fwd_x2(1)

    def f12():
        ag_fwd_sib("o", 1)

    def f13():
        ag_fwd_sib_g(1)
        down_have(1)

    forward(1, s["HSB"][...].astype(F32), (f10, none, f12, f13, none, none))
    ag_done()
    kv_done(0)
    kv_done(1)

    def c11():
        a0(1)
        a1(1)
        d1(1)
        b1("o", 1)

    def c12():
        a1b(1)

    load["cot"].wait()
    low = backward(1, s["HSB"][...].astype(F32), s["COTT"][...].astype(F32).T, (none, c11, c12, none))
    put_ig(1, low)
    b2("o", 1)

    def c00():
        a2(1)
        a0(0)
        a1(0)
        d1(0)
        b1("q", 1)

    def c01():
        b1("o", 0)

    def c02():
        a1b(0)
        d2(1)

    def c03():
        a3(1)
        b2("q", 1)
        b2("o", 0)

    low = backward(0, s["TOK"][...].astype(F32), s["IGB"][...].astype(F32), (c00, c01, c02, c03))
    put_ig(0, low)
    b1("q", 0)
    a2(0)
    a4(1)
    d3(1)
    b3("o", 1)
    b3("q", 1)
    b3("o", 0)
    d2(0)
    b2("q", 0)
    a3(0)
    d3(0)
    b3("q", 0)
    a5(1)
    b4("o", 1)
    b4("q", 1)
    b4("d", 1)
    a4(0)
    b4("o", 0)
    b4("d", 0)
    b4("q", 0)
    a5(0)
    grads_done()

    for m in ("g", "d", "o", "q", "kv", "ga", "gf"):
        store[m].wait()

    @pl.when(sec == 0)
    def _():
        store["hs0"].wait()
        store["ig0"].wait()
        hs_send(1).wait()
        ig_send(1).wait()

    @pl.when(sec == 1)
    def _():
        store["hs1"].wait()
        store["ig1"].wait()
        hs_send(0).wait()
        ig_send(0).wait()


def hand_on(*refs):
    n = 9
    sems = refs[-1]
    into = [pltpu.make_async_copy(refs[i], refs[2 * n + i], sems.at[0, i]) for i in range(n)]
    out = [pltpu.make_async_copy(refs[2 * n + i], refs[n + i], sems.at[1, i]) for i in range(n)]
    for copy in into:
        copy.start()
    for i in range(n):
        into[i].wait()
        out[i].start()
    for copy in out:
        copy.wait()


def body(tokens, cotangent, block_map, gain_a, w_q, w_kv, w_o, gain_f, w_gu, w_d):
    any_ = pl.BlockSpec(memory_space=pl.ANY)
    vm = pl.BlockSpec(memory_space=pltpu.VMEM)
    shapes = (
        jax.ShapeDtypeStruct((1, 2, D, R), BF),
        jax.ShapeDtypeStruct((1, 2, D, R), BF),
        jax.ShapeDtypeStruct((1, 72), F32),
        jax.ShapeDtypeStruct((1, 72, D), F32),
        jax.ShapeDtypeStruct((1, 72, 384), F32),
        jax.ShapeDtypeStruct((1, 72, D), F32),
        jax.ShapeDtypeStruct((1, 72), F32),
        jax.ShapeDtypeStruct((1, 72, 2 * FF), F32),
        jax.ShapeDtypeStruct((1, 192, D), F32),
    )
    outs = pl.pallas_call(
        mega,
        out_shape=shapes,
        in_specs=[any_, any_, pl.BlockSpec(memory_space=pltpu.SMEM), vm, vm] + [any_] * 5,
        out_specs=(any_,) * 9,
        scratch_shapes=[pltpu.VMEM(shape, dtype) for shape, dtype in SCRATCH.values()]
        + [pltpu.SemaphoreType.DMA((N_SEMS,))] * 2
        + [pltpu.SemaphoreType.REGULAR((6,)), pltpu.SemaphoreType.DMA((16,))],
        compiler_params=pltpu.CompilerParams(
            collective_id=0, has_side_effects=True, vmem_limit_bytes=64 * 2**20
        ),
        name="layers",
    )(tokens.swapaxes(1, 2), cotangent.swapaxes(1, 2), block_map, gain_a, gain_f, w_q, w_kv, w_o, w_gu, w_d)
    hs, ig, *grads = pl.pallas_call(
        hand_on,
        out_shape=shapes,
        in_specs=[any_] * 9,
        out_specs=(any_,) * 9,
        scratch_shapes=[pltpu.VMEM(a.shape, a.dtype) for a in shapes] + [pltpu.SemaphoreType.DMA((2, 9))],
        name="results",
    )(*outs)
    return (hs.swapaxes(2, 3), ig.swapaxes(2, 3), *grads)


def solution(mesh):
    torus = Mesh(mesh.devices.reshape(2, 4, 2, 4, 2), ("section", "z", "ylo", "x", "core"))
    return jax.shard_map(
        body,
        mesh=torus,
        in_specs=(
            P(DP, CONTEXT, None),
            P(DP, CONTEXT, None),
            P(DP, None),
            P("section", DP),
            P("section", DP, None),
            P("section", DP, None),
            P("section", DP, None),
            P("section", DP),
            P("section", DP, None),
            P("section", DP, None),
        ),
        out_specs=(
            P("section", DP, CONTEXT, None),
            P("section", DP, CONTEXT, None),
            P("section", DP),
            P("section", DP, None),
            P("section", DP, None),
            P("section", DP, None),
            P("section", DP),
            P("section", DP, None),
            P("section", DP, None),
        ),
        check_vma=False,
    )
```
